32 devices in a mesh: lon: 8 (over y, x, core), lat: 4 (over z).
Axes of the slice: x: 2, y: 2, z: 4, core: 2. Of those that a mesh axis runs over, the one named last changes fastest.
Arguments:
- ocean_state: float32 [4, 8, 2048, 512], P(None, None, 'lon', 'lat'), may hold values from -6 to 6
- diffusivity: float32 [7, 2048, 512], P(None, 'lon', 'lat'), may hold values from 0.05 to 2
- land_mask: int32 [2048, 512], P('lon', 'lat'), may hold values from 0 to 1, as said below
- tile_plan: int32 [16, 4], P(None, 'lat'), may hold values from 0 to 15, as said below
Outputs:
- moved_state: float32 [4, 8, 2048, 512], P(None, None, 'lon', 'lat')
The draws below stay inside these ranges and needn't reach their ends.
Inputs may be any that keep to these rules, and one draw needn't show every extreme that they name: `land_mask`: tiles of 128 x 128 columns may be land throughout; others are ocean throughout or mixed. Each column of tile_plan is a permutation of 0 to 15; a tile whose columns are all land keeps its position; every tile lands within 3 tile positions of where it stands, counted around the longitude loop; in some row one tile moves 3 positions east and one 3 positions west.
All inputs are finite; a program needn't handle non-finite values.
Results may differ from the reference program's by a relative error of at most 0.00002.
Values sent between devices are 32-bit elements; how exact they have to be, the bound alone decides.
A program may use at most 128 MiB of HBM per device.

```python
import math
import jax
import jax.numpy as jnp

TILE = 128
LEVELS = 8
NX = 2048
NY = 512


def shared_layout(key):
    tile_total = NX // TILE
    row_total = NY // TILE
    tile_kind = jax.random.randint(jax.random.fold_in(key, 11), (tile_total, row_total), 0, 10)
    forced_row = jax.random.randint(jax.random.fold_in(key, 12), (), 0, row_total)
    second_row = (forced_row + 1) % row_total
    third_row = (forced_row + 2) % row_total
    row_index = jnp.arange(row_total)[None, :]
    forced_cell = (row_index == forced_row) | (row_index == second_row) | (row_index == third_row)
    tile_kind = jnp.where(forced_cell, 9, tile_kind)
    return (tile_kind, forced_row, second_row, third_row)


def draw_land_mask(key, part):
    tile_kind, forced_row, second_row, third_row = shared_layout(key)
    kind_cells = jnp.repeat(jnp.repeat(tile_kind, TILE, axis=0), TILE, axis=1)
    coastal = jax.random.randint(jax.random.fold_in(key, 14), (NX, NY), 0, 2)
    return jnp.where(kind_cells < 3, 0, jnp.where(kind_cells < 6, coastal, 1)).astype(jnp.int32)


def draw_tile_plan(key, part):
    tile_kind, forced_row, second_row, third_row = shared_layout(key)
    tile_total = NX // TILE
    row_total = NY // TILE
    group_total = tile_total // 4
    row_index = jnp.arange(row_total)
    phase = jax.random.randint(jax.random.fold_in(key, 15), (row_total,), 0, 4)
    phase = jnp.where(row_index == forced_row, 1, jnp.where(row_index == second_row, 3, jnp.where(row_index == third_row, 0, phase)))
    rotated_index = jnp.arange(tile_total)[:, None]
    real_of_rotated = (rotated_index + phase[None, :]) % tile_total
    kind_rotated = jnp.take_along_axis(tile_kind, real_of_rotated, axis=0)
    ocean = (kind_rotated >= 3).astype(jnp.int32).reshape(group_total, 4, row_total)
    local_index = jnp.arange(4)
    raw_keys = jax.random.randint(jax.random.fold_in(key, 16), (group_total, 4, row_total), 0, 1 << 20) * 4 + local_index[None, :, None]
    forced_here = (row_index[None, None, :] == forced_row) | (row_index[None, None, :] == second_row) | (row_index[None, None, :] == third_row)
    forced_here = jnp.broadcast_to(forced_here, (group_total, 4, row_total))
    sort_keys = jnp.where(forced_here, 3 - local_index[None, :, None], raw_keys)
    lower_mask = (local_index[:, None] < local_index[None, :]).astype(jnp.int32)
    ocean_rank = jnp.sum(ocean[:, :, None, :] * lower_mask[None, :, :, None], axis=1)
    smaller = (sort_keys[:, :, None, :] < sort_keys[:, None, :, :]).astype(jnp.int32)
    perm_rank = jnp.sum(ocean[:, :, None, :] * smaller, axis=1)
    match = (ocean[:, None, :, :] == 1) & (ocean_rank[:, None, :, :] == perm_rank[:, :, None, :])
    target_local = jnp.sum(match.astype(jnp.int32) * local_index[None, None, :, None], axis=2)
    target_local = jnp.where(ocean == 1, target_local, local_index[None, :, None])
    group_base = 4 * jnp.arange(group_total)[:, None, None]
    target_rotated = (group_base + target_local).reshape(tile_total, row_total)
    target_real = (target_rotated + phase[None, :]) % tile_total
    real_index = jnp.arange(tile_total)[:, None]
    rotated_of_real = (real_index - phase[None, :]) % tile_total
    return jnp.take_along_axis(target_real, rotated_of_real, axis=0).astype(jnp.int32)


def block_levels(rng, dims, cuts, low, largest):
    gain = 1.0
    for axis_at, parts in cuts:
        draws = jax.random.uniform(jax.random.fold_in(jax.random.fold_in(rng, 6), axis_at), (parts,), jnp.float32, low / len(cuts), largest / len(cuts))
        gain = gain * jnp.repeat(jnp.exp(draws), dims[axis_at] // parts).reshape((-1,) + (1,) * (len(dims) - 1 - axis_at))
    return gain


def normal_values(stream_key, dims, width, bound, split=(), kind=jnp.bfloat16):
    loudness = block_levels(stream_key, dims, split, -0.22, 0.18) if split else 1.0
    values = jax.random.normal(stream_key, dims, jnp.float32) * width * loudness
    return jnp.minimum(jnp.maximum(values, -bound), bound).astype(kind)


def setup_inputs(seed: int = 0) -> dict:
    seeds = jax.random.split(jax.random.key(seed), 5)
    ocean_state = normal_values(seeds[0], (4, LEVELS, NX, NY), 1.0, 6.0, ((2, 8), (3, 4)), jnp.float32)
    diffusivity = jnp.clip(jnp.exp(math.log(2.0) - 3.6888794 * jax.random.uniform(seeds[1], (LEVELS - 1, NX, NY), jnp.float32) ** block_levels(seeds[1], (LEVELS - 1, NX, NY), ((1, 8), (2, 4)), -0.2, 0.2)), 0.05, 2.0)
    land_mask = draw_land_mask(jax.random.fold_in(seeds[4], 71), 0)
    tile_plan = draw_tile_plan(jax.random.fold_in(seeds[4], 71), 0)
    return {"ocean_state": ocean_state, "diffusivity": diffusivity, "land_mask": land_mask, "tile_plan": tile_plan}


advect_coef = 0.1
diffuse_coef = 0.1
gradient_coef = 0.1
thermal_coef = 0.2
haline_coef = 0.15
weight_coef = 0.25
mixing_coef = 1.0


def tendency(padded, wet_mask):
    center = padded[:, :, 1:-1, 1:-1]
    east_cells = padded[:, :, 2:, 1:-1]
    west_cells = padded[:, :, :-2, 1:-1]
    north_cells = padded[:, :, 1:-1, 2:]
    south_cells = padded[:, :, 1:-1, :-2]
    density = haline_coef * padded[1] - thermal_coef * padded[0]
    pressure = weight_coef * jnp.cumsum(density, axis=0)
    zonal_gradient = pressure[:, 2:, 1:-1] - pressure[:, :-2, 1:-1]
    merid_gradient = pressure[:, 1:-1, 2:] - pressure[:, 1:-1, :-2]
    zonal_flow = center[2]
    meridional = center[3]
    advect = -advect_coef * (zonal_flow * (east_cells - west_cells) + meridional * (north_cells - south_cells))
    diffuse = diffuse_coef * (east_cells + west_cells + north_cells + south_cells - 4.0 * center)
    updated = center + advect + diffuse
    updated = updated.at[2].add(-gradient_coef * zonal_gradient)
    updated = updated.at[3].add(-gradient_coef * merid_gradient)
    return updated * wet_mask


def mix_columns(fields, diffusivity):
    levels = fields.shape[1]
    zero_band = jnp.zeros_like(diffusivity[0])
    lower_band = [zero_band] + [-mixing_coef * diffusivity[level_index - 1] for level_index in range(1, levels)]
    upper_band = [-mixing_coef * diffusivity[level_index] for level_index in range(levels - 1)] + [zero_band]
    sweep_upper = []
    sweep_rhs = []
    for level_index in range(levels):
        pivot_value = 1.0 - lower_band[level_index] - upper_band[level_index]
        rhs_level = fields[:, level_index]
        if level_index > 0:
            pivot_value = pivot_value - lower_band[level_index] * sweep_upper[level_index - 1]
            rhs_level = rhs_level - lower_band[level_index] * sweep_rhs[level_index - 1]
        sweep_upper.append(upper_band[level_index] / pivot_value)
        sweep_rhs.append(rhs_level / pivot_value)
    solution = [sweep_rhs[-1]]
    for level_index in range(levels - 2, -1, -1):
        solution.insert(0, sweep_rhs[level_index] - sweep_upper[level_index] * solution[0])
    return jnp.stack(solution, axis=1)


def fold_pad(fields):
    fold_signs = jnp.array([1.0, 1.0, -1.0, -1.0], jnp.float32)[:, None, None]
    lon_padded = jnp.concatenate([fields[:, :, -1:], fields, fields[:, :, :1]], axis=2)
    top_row = fields[:, :, ::-1, -1] * fold_signs
    corner_zero = jnp.zeros_like(top_row[:, :, :1])
    top_row = jnp.concatenate([corner_zero, top_row, corner_zero], axis=2)
    bottom_row = jnp.zeros_like(top_row)
    return jnp.concatenate([bottom_row[:, :, :, None], lon_padded, top_row[:, :, :, None]], axis=3)


def reference(ocean_state, diffusivity, land_mask, tile_plan):
    wet_mask = land_mask.astype(jnp.float32)
    fields = ocean_state * wet_mask
    padded = fold_pad(fields)
    stepped = tendency(padded, wet_mask)
    mixed_fields = mix_columns(stepped, diffusivity) * wet_mask
    tile_count = tile_plan.shape[0]
    row_count = tile_plan.shape[1]
    field_count = mixed_fields.shape[0]
    levels = mixed_fields.shape[1]
    total_x = mixed_fields.shape[2]
    tile_width = total_x // tile_count
    band_height = mixed_fields.shape[3] // row_count
    pieces = []
    for row_index in range(row_count):
        lat_band = mixed_fields[:, :, :, row_index * band_height:(row_index + 1) * band_height]
        lat_band = lat_band.reshape(field_count, levels, tile_count, tile_width, band_height)
        placed = jnp.zeros_like(lat_band).at[:, :, tile_plan[:, row_index]].set(lat_band)
        pieces.append(placed.reshape(field_count, levels, total_x, band_height))
    return jnp.concatenate(pieces, axis=3)
```

```python
import functools

import jax
import jax.numpy as jnp
from jax import lax
from jax.experimental import pallas as pl
from jax.experimental.pallas import tpu as pltpu
from jax.sharding import PartitionSpec as P

advect_coef = 0.1
diffuse_coef = 0.1
gradient_coef = 0.1
thermal_coef = 0.2
haline_coef = 0.15
weight_coef = 0.25

F32 = jnp.float32
MIB = 1 << 20
MESH = pl.DeviceIdType.MESH
STEP = 8
RELAYED = ((1, 4), (2,))


def remote_copy(source, target, send, recv, who):
    return pltpu.make_async_remote_copy(
        src_ref=source, dst_ref=target, send_sem=send, recv_sem=recv, device_id=who, device_id_type=MESH
    )


def halo_kernel(
    relays,
    plan_ref,
    state_ref,
    mask_ref,
    lat_ref,
    west_ref,
    east_ref,
    branch_ref,
    held,
    mask,
    lat_pack,
    lon_pack,
    north_in,
    south_in,
    west_in,
    east_in,
    count,
    counts_in,
    load_sem,
    send_sem,
    recv_sem,
):
    fields, levels, rows, lanes = held.shape
    half = rows // 2
    lane = lax.broadcasted_iota(jnp.int32, (8, lanes), 1)
    devices, bands = lax.axis_size("lon"), lax.axis_size("lat")
    lon, lat = lax.axis_index("lon"), lax.axis_index("lat")
    top = lat == bands - 1
    to_east = {"lon": lax.rem(lon + 1, devices)}
    to_west = {"lon": lax.rem(lon + devices - 1, devices)}
    across = {"lon": devices - 1 - lon}
    others = [{"lat": lax.rem(lat + o, bands)} for o in range(1, bands)]
    barrier = pltpu.get_barrier_semaphore()
    for who in [to_east, to_west, across] + others:
        pl.semaphore_signal(barrier, inc=1, device_id=who, device_id_type=MESH)

    mask_load = pltpu.make_async_copy(mask_ref, mask, load_sem.at[fields])
    mask_load.start()
    loads = [pltpu.make_async_copy(state_ref.at[f], held.at[f], load_sem.at[f]) for f in range(fields)]
    for load in loads:
        load.start()

    chips = devices // 2

    def leaving(chip, most):
        for way in (1, -1):
            number = jnp.int32(0)
            for t in range(4):
                number = number + leaves(plan_ref, chips, chip, t, way).astype(jnp.int32)
            most = jnp.maximum(most, number)
        return most

    most = lax.fori_loop(0, chips, leaving, jnp.int32(0))
    count[...] = jnp.full(count.shape, most, jnp.int32)
    mask_load.wait()
    first = mask[0:1, :].astype(F32)
    final = mask[rows - 1 : rows, :].astype(F32)
    for f in range(fields):
        loads[f].wait()

        def group(g, _):
            to = pl.ds(pl.multiple_of(g * 8, 8), 8)
            part = lat_pack[to, :] if f > 0 else jnp.zeros((8, lanes), F32)
            for slot in range(2):
                at = pl.ds(pl.multiple_of(slot * half + g * 8, 8), 8)
                wet = mask[at, :].astype(F32)
                for k in range(levels):
                    place = 64 * slot + 2 * (f * levels + k)
                    x = pltpu.roll(held[f, k, at, :] * wet, place + 1, 1)
                    part = jnp.where((lane >> 1) == (place >> 1), x, part)
            lat_pack[to, :] = part
            return 0

        lax.fori_loop(0, half // 8, group, 0, unroll=2)
        at_field = slice(f * levels, (f + 1) * levels)
        lon_pack[0, at_field, :] = jnp.concatenate([held[f, k, 0:1, :] for k in range(levels)], 0) * first
        lon_pack[1, at_field, :] = (
            jnp.concatenate([held[f, k, rows - 1 : rows, :] for k in range(levels)], 0) * final
        )

    pl.semaphore_wait(barrier, 3 + bands - 1)

    def remote(source, target, at, recv_at, who):
        return remote_copy(source, target, send_sem.at[at], recv_sem.at[recv_at], who)

    up = remote(lat_pack, south_in, 0, 0, {"lat": jnp.minimum(lat + 1, bands - 1)})
    down = remote(lat_pack, north_in, 1, 1, {"lat": jnp.maximum(lat - 1, 0)})
    fold = remote(lat_pack, north_in, 0, 1, across)
    east = remote(lon_pack.at[1], west_in, 2, 2, to_east)
    west = remote(lon_pack.at[0], east_in, 3, 3, to_west)
    tell = [remote(count, counts_in.at[o], 4 + o, 4 + o, who) for o, who in enumerate(others)]
    pl.when(top)(fold.start)
    pl.when(jnp.logical_not(top))(up.start)
    pl.when(lat > 0)(down.start)
    for t in tell:
        t.start()
    east.start()
    west.start()

    values = [count[...]]
    value_rows = [lat]
    for o, t in enumerate(tell):
        t.wait_recv()
        values.append(counts_in[o])
        value_rows.append(lax.rem(lat + bands - o - 1, bands))
    largest, idle = values[0], jnp.full(count.shape, bands, jnp.int32)
    for value, row in zip(values, value_rows):
        largest = jnp.maximum(largest, value)
        idle = jnp.minimum(idle, jnp.where(value == 0, row, bands))
    if relays:
        branch = jnp.where(largest <= 1, idle, bands - 1 + largest)
    else:
        branch = jnp.maximum(largest, 1) - 1
    branch_ref[0] = jnp.max(branch)
    east.wait_recv()
    west_ref[...] = west_in[...]
    west.wait_recv()
    east_ref[...] = east_in[...]

    @pl.when(lat > 0)
    def _():
        up.wait_recv()

    @pl.when(lat == 0)
    def _():
        south_in[...] = jnp.zeros_like(south_in)

    down.wait_recv()
    place = lax.broadcasted_iota(jnp.int32, (half, lanes), 1)
    south = pltpu.roll(south_in[...], 2, 1)

    @pl.when(top)
    def _():
        r = lax.broadcasted_iota(jnp.int32, (half, half), 0)
        c = lax.broadcasted_iota(jnp.int32, (half, half), 1)
        turn = jnp.where(r + c == half - 1, 1.0, 0.0).astype(F32)
        mirror = jnp.dot(turn, north_in[...], precision=lax.Precision.HIGHEST, preferred_element_type=F32)
        mirror = pltpu.roll(mirror, 65, 1)
        mirror = jnp.where((place & 63) >= 32, -mirror, mirror)
        lat_ref[...] = jnp.where((place & 1) == 1, mirror, south)

    @pl.when(jnp.logical_not(top))
    def _():
        lat_ref[...] = jnp.where((place & 1) == 1, north_in[...], south)

    up.wait_send()
    pl.when(lat > 0)(down.wait_send)
    east.wait_send()
    west.wait_send()
    for t in tell:
        t.wait_send()


def halos(relays, plan, state, mask):
    fields, levels, rows, lanes = state.shape
    bands = lax.axis_size("lat")
    pack = (rows // 2, lanes)
    edge = (fields * levels, lanes)
    near = pl.BlockSpec(memory_space=pltpu.VMEM)
    anywhere = pl.BlockSpec(memory_space=pl.ANY)
    scalars = pl.BlockSpec(memory_space=pltpu.SMEM)
    return pl.pallas_call(
        functools.partial(halo_kernel, relays),
        in_specs=[scalars, anywhere, anywhere],
        out_specs=[near, near, near, scalars],
        out_shape=[
            jax.ShapeDtypeStruct(pack, F32),
            jax.ShapeDtypeStruct(edge, F32),
            jax.ShapeDtypeStruct(edge, F32),
            jax.ShapeDtypeStruct((1,), jnp.int32),
        ],
        scratch_shapes=[
            pltpu.VMEM(state.shape, F32),
            pltpu.VMEM(mask.shape, jnp.int32),
            pltpu.VMEM(pack, F32),
            pltpu.VMEM((2,) + edge, F32),
            pltpu.VMEM(pack, F32),
            pltpu.VMEM(pack, F32),
            pltpu.VMEM(edge, F32),
            pltpu.VMEM(edge, F32),
            pltpu.VMEM((8, lanes), jnp.int32),
            pltpu.VMEM((bands - 1, 8, lanes), jnp.int32),
            pltpu.SemaphoreType.DMA((fields + 1,)),
            pltpu.SemaphoreType.DMA((4 + bands - 1,)),
            pltpu.SemaphoreType.DMA((4 + bands - 1,)),
        ],
        compiler_params=pltpu.CompilerParams(
            collective_id=0, has_side_effects=True, vmem_limit_bytes=16 * MIB
        ),
    )(plan, state, mask)


def leaves(plan_ref, chips, chip, t, way):
    target = plan_ref[4 * chip + t] // 4
    return target == lax.rem(chip + way + chips, chips)


def pick(index, values):
    chosen = values[0]
    for at, value in enumerate(values[1:], 1):
        chosen = jnp.where(index == at, value, chosen)
    return chosen


def move_kernel(
    rounds,
    idle,
    plan_ref,
    state_ref,
    diff_ref,
    mask_ref,
    lat_ref,
    west_ref,
    east_ref,
    out_ref,
    padded,
    wet,
    mine,
    theirs,
    other,
    other_theirs,
    leaving,
    arrived,
    swapped,
    relayed,
    result,
    load_sem,
    store_sem,
    half_send,
    half_recv,
    tile_send,
    tile_recv,
    swap_send,
    swap_recv,
    relay_send,
    relay_recv,
):
    fields, levels, rows, lanes = state_ref.shape
    planes = fields * levels
    quarter = rows // 4
    chunks = quarter // STEP
    devices, bands = lax.axis_size("lon"), lax.axis_size("lat")
    chips = devices // 2
    tiles = 4 * chips
    lon, lat = lax.axis_index("lon"), lax.axis_index("lat")
    chip, core = lon // 2, lax.rem(lon, 2)
    twin = {"lon": lon + 1 - 2 * core}
    ahead_lon = lax.rem(lon + 2, devices)
    behind_lon = lax.rem(lon + devices - 2, devices)
    ways = ((1, ahead_lon), (-1, behind_lon))
    keys = [(side, r) for side in range(2) for r in range(rounds)]
    active = None if idle is None else lat != idle

    def busy(work):
        if idle is None:
            work()
        else:
            pl.when(active)(work)

    def resting(work):
        if idle is not None:
            pl.when(lat == idle)(work)

    loads = [
        pltpu.make_async_copy(state_ref.at[f], padded.at[f, :, pl.ds(8, rows), :], load_sem.at[f])
        for f in range(fields)
    ]
    barrier = pltpu.get_barrier_semaphore()

    def greet(who):
        pl.semaphore_signal(barrier, inc=1, device_id=who, device_id_type=MESH)

    greet(twin)

    @busy
    def _():
        greet({"lon": ahead_lon})
        greet({"lon": behind_lon})
        if idle is not None:
            for at in (lon, ahead_lon, behind_lon):
                greet({"lat": idle, "lon": at})

    @resting
    def _():
        for o in range(1, bands):
            for at in (lon, ahead_lon, behind_lon):
                greet({"lat": (idle + o) % bands, "lon": at})

    for load in loads:
        load.start()

    wet[pl.ds(8, rows), :] = mask_ref[...].astype(F32)
    wet[0:8, :] = jnp.ones((8, lanes), F32)
    wet[rows + 8 : rows + 16, :] = jnp.ones((8, lanes), F32)
    for f in range(fields):
        for k in range(levels):
            i = f * levels + k
            padded[f, k, 7:8, :] = west_ref[i : i + 1, :]
            padded[f, k, rows + 8 : rows + 9, :] = east_ref[i : i + 1, :]

    chosen = {}
    for side, (way, _) in enumerate(ways):
        hits = [leaves(plan_ref, chips, chip, t, way) for t in range(4)]
        for r in range(rounds):
            count, tile = jnp.int32(0), jnp.int32(0)
            for t in range(4):
                tile = jnp.where(hits[t] & (count == r), t, tile)
                count = count + hits[t].astype(jnp.int32)
            chosen[side, r] = jnp.where(tile // 2 == core, 0, 2) + lax.rem(tile, 2)

    lane = lax.broadcasted_iota(jnp.int32, (STEP, lanes), 1)
    is_last = lane == lanes - 1
    is_first = lane == 0
    force = gradient_coef * weight_coef

    def solve(c, half, to_ref):
        def group(slot, _):
            row = pl.multiple_of(half * quarter + c * STEP, STEP)
            base = pl.multiple_of(slot * (2 * quarter) + row, STEP)
            edges = pltpu.roll(lat_ref[pl.ds(row, STEP), :], 64 * slot, 1)
            wet_c = wet[pl.ds(base + 8, STEP), :]
            wet_e = wet[pl.ds(base + 9, STEP), :]
            wet_w = wet[pl.ds(base + 7, STEP), :]
            zonal = meridional = None
            upper = []
            rhs = []
            for k in range(levels):
                center = [padded[f, k, pl.ds(base + 8, STEP), :] * wet_c for f in range(fields)]
                u, v = center[2], center[3]
                grad_x, grad_y, value = [], [], []
                for f in range(fields):
                    i = f * levels + k
                    e = padded[f, k, pl.ds(base + 9, STEP), :] * wet_e
                    w = padded[f, k, pl.ds(base + 7, STEP), :] * wet_w
                    edge = pltpu.roll(edges, (lanes - 2 - 2 * i) % lanes, 1)
                    n = jnp.where(is_last, edge, pltpu.roll(center[f], lanes - 1, 1))
                    s = jnp.where(is_first, edge, pltpu.roll(center[f], 1, 1))
                    gx, gy = e - w, n - s
                    grad_x.append(gx)
                    grad_y.append(gy)
                    total = (e + w) + (n + s)
                    flow = u * gx + v * gy
                    value.append(
                        (1.0 - 4.0 * diffuse_coef) * center[f] + (diffuse_coef * total - advect_coef * flow)
                    )
                dx = (force * haline_coef) * grad_x[1] - (force * thermal_coef) * grad_x[0]
                dy = (force * haline_coef) * grad_y[1] - (force * thermal_coef) * grad_y[0]
                zonal = dx if k == 0 else zonal + dx
                meridional = dy if k == 0 else meridional + dy
                value[2] = value[2] - zonal
                value[3] = value[3] - meridional
                lower_k = diff_ref[k - 1, pl.ds(base, STEP), :] if k > 0 else None
                upper_k = diff_ref[k, pl.ds(base, STEP), :] if k < levels - 1 else None
                pivot = 1.0
                if k > 0:
                    pivot = pivot + lower_k
                if k < levels - 1:
                    pivot = pivot + upper_k
                if k > 0:
                    pivot = pivot - lower_k * upper[k - 1]
                inverse = 1.0 / pivot
                upper.append(upper_k * inverse if k < levels - 1 else None)
                if k > 0:
                    value = [value[f] + lower_k * rhs[k - 1][f] for f in range(fields)]
                rhs.append([value[f] * inverse for f in range(fields)])
            for f in range(fields):
                x = rhs[levels - 1][f]
                to_ref[c, slot, f * levels + levels - 1] = x * wet_c
                for k in range(levels - 2, -1, -1):
                    x = rhs[k][f] + upper[k] * x
                    to_ref[c, slot, f * levels + k] = x * wet_c
            return 0

        lax.fori_loop(0, 2, group, 0)

    def first(c):
        return remote_copy(theirs.at[c], other.at[c], half_send.at[c, 0], half_recv.at[c, 0], twin)

    def second(c):
        return remote_copy(mine.at[c], other_theirs.at[c], half_send.at[c, 1], half_recv.at[c, 1], twin)

    def direct(c, side, r):
        return remote_copy(
            leaving.at[side, r, c],
            arrived.at[side, r, c],
            tile_send.at[c, side, r],
            tile_recv.at[c, side, r],
            {"lon": ways[side][1]},
        )

    def swap(c, side, r):
        return remote_copy(
            arrived.at[side, r, c],
            swapped.at[side, r, c],
            swap_send.at[c, side, r],
            swap_recv.at[c, side, r],
            twin,
        )

    stops = [(side, n, c) for side, cs in enumerate(RELAYED) for n, c in enumerate(cs)] if idle is not None else []
    stops.sort(key=lambda stop: stop[2])

    def detour(at, side, c):
        j = lax.rem(lat - (idle + 1) + 2 * bands, bands)
        return remote_copy(
            leaving.at[side, 0, c],
            relayed.at[j, at],
            tile_send.at[c, side, 0],
            relay_recv.at[j, at],
            {"lat": idle, "lon": ways[side][1]},
        )

    def forward(j, at, side, c):
        return remote_copy(
            relayed.at[j, at],
            arrived.at[side, 0, c],
            relay_send.at[j, at],
            tile_recv.at[c, side, 0],
            {"lat": (idle + 1 + j) % bands},
        )

    for load in loads:
        load.wait()

    def advance(c, _):
        solve(c, 1 - core, theirs)

        @pl.when(c == 0)
        def _():
            if idle is None:
                pl.semaphore_wait(barrier, 3)
            else:
                busy(lambda: pl.semaphore_wait(barrier, 6))
                resting(lambda: pl.semaphore_wait(barrier, 1 + 3 * (bands - 1)))

        first(c).start()
        solve(c, core, mine)

        @busy
        def _():
            first(c).wait_recv()

            def pack(i, _):
                held = [ref[c, slot, i] for ref in (mine, other) for slot in range(2)]
                for (side, r), index in chosen.items():
                    leaving[side, r, c, i] = pick(index, held)
                return 0

            lax.fori_loop(0, planes, pack, 0, unroll=8)
            for side, r in keys:
                around = [c == stop[2] for stop in stops if stop[0] == side]
                if around:
                    pl.when(jnp.logical_not(functools.reduce(jnp.logical_or, around)))(direct(c, side, r).start)
                else:
                    direct(c, side, r).start()
            for at, (side, _, when) in enumerate(stops):
                pl.when(c == when)(detour(at, side, when).start)

        second(c).start()
        return 0

    lax.fori_loop(0, chunks, advance, 0)

    @resting
    def _():
        for at, (side, _, c) in enumerate(stops):
            for j in range(bands - 1):
                remote_copy(
                    relayed.at[j, at], relayed.at[j, at], relay_send.at[j, at], relay_recv.at[j, at], twin
                ).wait_recv()
                forward(j, at, side, c).start()

    origin = []
    for slot in range(2):
        target = 2 * lon + slot
        source = jnp.int32(0)
        for shift in range(-3, 4):
            g = lax.rem(target + shift + tiles, tiles)
            source = jnp.where(plan_ref[g] == target, g, source)
        from_chip, t = source // 4, lax.rem(source, 4)
        at = jnp.where(t // 2 == core, 0, 2) + lax.rem(t, 2)
        for side, (way, _) in enumerate(ways):
            came = from_chip == lax.rem(chip - way + chips, chips)
            rank = jnp.int32(0)
            for q in range(3):
                hit = leaves(plan_ref, chips, from_chip, q, way) & (q < t)
                rank = rank + hit.astype(jnp.int32)
            at = jnp.where(came, 4 + side * rounds + jnp.minimum(rank, rounds - 1), at)
        origin.append(at)

    def store(c, slot, part):
        half = core if part == 0 else 1 - core
        row = pl.multiple_of(2 * quarter * slot + half * quarter + c * STEP, STEP)
        return pltpu.make_async_copy(
            result.at[c, slot, part], out_ref.at[:, :, pl.ds(row, STEP), :], store_sem.at[c, slot, part]
        )

    def place(c):
        second(c).wait_recv()
        resting(first(c).wait_recv)

        @busy
        def _():
            for key in keys:
                swap(c, *key).wait_recv()

        def level(k, _):
            for f in range(fields):
                i = f * levels + k
                for part in range(2):
                    near, far, came = (
                        (mine, other, arrived) if part == 0 else (theirs, other_theirs, swapped)
                    )
                    values = [ref[c, slot, i] for ref in (near, far) for slot in range(2)]
                    values += [came[side, r, c, i] for side, r in keys]
                    for slot in range(2):
                        result[c, slot, part, f, k] = pick(origin[slot], values)
            return 0

        lax.fori_loop(0, levels, level, 0)
        for slot in range(2):
            for part in range(2):
                store(c, slot, part).start()

    def drain(c, _):
        @busy
        def _():
            for key in keys:
                direct(c, *key).wait_recv()
                swap(c, *key).start()

        @pl.when(c > 0)
        def _():
            place(c - 1)

        return 0

    lax.fori_loop(0, chunks, drain, 0)
    place(chunks - 1)

    def finish(c, _):
        first(c).wait_send()
        second(c).wait_send()

        @busy
        def _():
            for key in keys:
                direct(c, *key).wait_send()
                swap(c, *key).wait_send()

        for slot in range(2):
            for part in range(2):
                store(c, slot, part).wait()
        return 0

    lax.fori_loop(0, chunks, finish, 0)

    @resting
    def _():
        for at, (side, _, c) in enumerate(stops):
            for j in range(bands - 1):
                forward(j, at, side, c).wait_send()


def move(rounds, idle, plan, state, diffusivity, mask, lat_edges, west, east):
    fields, levels, rows, lanes = state.shape
    bands = lax.axis_size("lat")
    chunks = rows // 4 // STEP
    planes = fields * levels
    stops = sum(len(cs) for cs in RELAYED)
    anywhere = pl.BlockSpec(memory_space=pl.ANY)
    near = pl.BlockSpec(memory_space=pltpu.VMEM)
    halves = pltpu.VMEM((chunks, 2, planes, STEP, lanes), F32)
    pieces = pltpu.VMEM((2, rounds, chunks, planes, STEP, lanes), F32)
    relay_shape = (bands - 1, stops) if idle is not None else (1, 1)
    dma = pltpu.SemaphoreType.DMA
    number = rounds if idle is None else 4 + idle
    return pl.pallas_call(
        functools.partial(move_kernel, rounds, idle),
        in_specs=[pl.BlockSpec(memory_space=pltpu.SMEM), anywhere] + [near] * 5,
        out_specs=anywhere,
        out_shape=jax.ShapeDtypeStruct(state.shape, F32),
        scratch_shapes=[
            pltpu.VMEM((fields, levels, rows + 16, lanes), F32),
            pltpu.VMEM((rows + 16, lanes), F32),
            halves,
            halves,
            halves,
            halves,
            pieces,
            pieces,
            pieces,
            pltpu.VMEM(relay_shape + (planes, STEP, lanes), F32),
            pltpu.VMEM((chunks, 2, 2, fields, levels, STEP, lanes), F32),
            dma((fields,)),
            dma((chunks, 2, 2)),
            dma((chunks, 2)),
            dma((chunks, 2)),
            dma((chunks, 2, rounds)),
            dma((chunks, 2, rounds)),
            dma((chunks, 2, rounds)),
            dma((chunks, 2, rounds)),
            dma(relay_shape),
            dma(relay_shape),
        ],
        compiler_params=pltpu.CompilerParams(
            collective_id=number, has_side_effects=True, vmem_limit_bytes=(24 + 6 * rounds) * MIB
        ),
    )(plan, state, diffusivity, mask, lat_edges, west, east)


def local(relays, state, diffusivity, mask, tile_plan):
    plan = tile_plan.reshape(-1)
    lat_edges, west, east, branch = halos(relays, plan, state, mask)
    branches = [functools.partial(move, rounds, None) for rounds in (1, 2, 3)]
    if relays:
        branches = [functools.partial(move, 1, row) for row in range(lax.axis_size("lat"))] + branches
    return lax.switch(branch[0], branches, plan, state, diffusivity, mask, lat_edges, west, east)


def solution(mesh):
    placed = (P(None, None, "lon", "lat"), P(None, "lon", "lat"), P("lon", "lat"), P(None, "lat"))
    relays = False
    return jax.shard_map(
        functools.partial(local, relays),
        mesh=mesh,
        in_specs=placed,
        out_specs=P(None, None, "lon", "lat"),
        check_vma=False,
    )
```

```python
import functools

import jax
import jax.numpy as jnp
from jax import lax
from jax.experimental import pallas as pl
from jax.experimental.pallas import tpu as pltpu
from jax.sharding import PartitionSpec as P

advect_coef = 0.1
diffuse_coef = 0.1
gradient_coef = 0.1
thermal_coef = 0.2
haline_coef = 0.15
weight_coef = 0.25

F32 = jnp.float32
MIB = 1 << 20
MESH = pl.DeviceIdType.MESH
STEP = 8
RELAYED = 2


def remote_copy(source, target, send, recv, who):
    return pltpu.make_async_remote_copy(
        src_ref=source, dst_ref=target, send_sem=send, recv_sem=recv, device_id=who, device_id_type=MESH
    )


def halo_kernel(
    relays,
    plan_ref,
    state_ref,
    mask_ref,
    lat_ref,
    west_ref,
    east_ref,
    branch_ref,
    held,
    mask,
    lat_pack,
    lon_pack,
    north_in,
    south_in,
    west_in,
    east_in,
    count,
    counts_in,
    load_sem,
    send_sem,
    recv_sem,
):
    fields, levels, rows, lanes = held.shape
    half = rows // 2
    lane = lax.broadcasted_iota(jnp.int32, (8, lanes), 1)
    devices, bands = lax.axis_size("lon"), lax.axis_size("lat")
    lon, lat = lax.axis_index("lon"), lax.axis_index("lat")
    top = lat == bands - 1
    to_east = {"lon": lax.rem(lon + 1, devices)}
    to_west = {"lon": lax.rem(lon + devices - 1, devices)}
    across = {"lon": devices - 1 - lon}
    others = [{"lat": lax.rem(lat + o, bands)} for o in range(1, bands)]
    barrier = pltpu.get_barrier_semaphore()
    for who in [to_east, to_west, across] + others:
        pl.semaphore_signal(barrier, inc=1, device_id=who, device_id_type=MESH)

    mask_load = pltpu.make_async_copy(mask_ref, mask, load_sem.at[fields])
    mask_load.start()
    loads = [pltpu.make_async_copy(state_ref.at[f], held.at[f], load_sem.at[f]) for f in range(fields)]
    for load in loads:
        load.start()

    chips = devices // 2

    def leaving(chip, most):
        for way in (1, -1):
            number = jnp.int32(0)
            for t in range(4):
                number = number + leaves(plan_ref, chips, chip, t, way).astype(jnp.int32)
            most = jnp.maximum(most, number)
        return most

    most = lax.fori_loop(0, chips, leaving, jnp.int32(0))
    count[...] = jnp.full(count.shape, most, jnp.int32)
    mask_load.wait()
    first = mask[0:1, :].astype(F32)
    final = mask[rows - 1 : rows, :].astype(F32)
    for f in range(fields):
        loads[f].wait()

        def group(g, _):
            to = pl.ds(pl.multiple_of(g * 8, 8), 8)
            part = lat_pack[to, :] if f > 0 else jnp.zeros((8, lanes), F32)
            for slot in range(2):
                at = pl.ds(pl.multiple_of(slot * half + g * 8, 8), 8)
                wet = mask[at, :].astype(F32)
                for k in range(levels):
                    place = 64 * slot + 2 * (f * levels + k)
                    x = pltpu.roll(held[f, k, at, :] * wet, place + 1, 1)
                    part = jnp.where((lane >> 1) == (place >> 1), x, part)
            lat_pack[to, :] = part
            return 0

        lax.fori_loop(0, half // 8, group, 0, unroll=2)
        at_field = slice(f * levels, (f + 1) * levels)
        lon_pack[0, at_field, :] = jnp.concatenate([held[f, k, 0:1, :] for k in range(levels)], 0) * first
        lon_pack[1, at_field, :] = (
            jnp.concatenate([held[f, k, rows - 1 : rows, :] for k in range(levels)], 0) * final
        )

    pl.semaphore_wait(barrier, 3 + bands - 1)

    def remote(source, target, at, recv_at, who):
        return remote_copy(source, target, send_sem.at[at], recv_sem.at[recv_at], who)

    up = remote(lat_pack, south_in, 0, 0, {"lat": jnp.minimum(lat + 1, bands - 1)})
    down = remote(lat_pack, north_in, 1, 1, {"lat": jnp.maximum(lat - 1, 0)})
    fold = remote(lat_pack, north_in, 0, 1, across)
    east = remote(lon_pack.at[1], west_in, 2, 2, to_east)
    west = remote(lon_pack.at[0], east_in, 3, 3, to_west)
    tell = [remote(count, counts_in.at[o], 4 + o, 4 + o, who) for o, who in enumerate(others)]
    pl.when(top)(fold.start)
    pl.when(jnp.logical_not(top))(up.start)
    pl.when(lat > 0)(down.start)
    for t in tell:
        t.start()
    east.start()
    west.start()

    values = [count[...]]
    value_rows = [lat]
    for o, t in enumerate(tell):
        t.wait_recv()
        values.append(counts_in[o])
        value_rows.append(lax.rem(lat + bands - o - 1, bands))
    largest, idle = values[0], jnp.full(count.shape, bands, jnp.int32)
    for value, row in zip(values, value_rows):
        largest = jnp.maximum(largest, value)
        idle = jnp.minimum(idle, jnp.where(value == 0, row, bands))
    if relays:
        branch = jnp.where(largest <= 1, idle, bands - 1 + largest)
    else:
        branch = jnp.maximum(largest, 1) - 1
    branch_ref[0] = jnp.max(branch)
    east.wait_recv()
    west_ref[...] = west_in[...]
    west.wait_recv()
    east_ref[...] = east_in[...]

    @pl.when(lat > 0)
    def _():
        up.wait_recv()

    @pl.when(lat == 0)
    def _():
        south_in[...] = jnp.zeros_like(south_in)

    down.wait_recv()
    place = lax.broadcasted_iota(jnp.int32, (half, lanes), 1)
    south = pltpu.roll(south_in[...], 2, 1)

    @pl.when(top)
    def _():
        r = lax.broadcasted_iota(jnp.int32, (half, half), 0)
        c = lax.broadcasted_iota(jnp.int32, (half, half), 1)
        turn = jnp.where(r + c == half - 1, 1.0, 0.0).astype(F32)
        mirror = jnp.dot(turn, north_in[...], precision=lax.Precision.HIGHEST, preferred_element_type=F32)
        mirror = pltpu.roll(mirror, 65, 1)
        mirror = jnp.where((place & 63) >= 32, -mirror, mirror)
        lat_ref[...] = jnp.where((place & 1) == 1, mirror, south)

    @pl.when(jnp.logical_not(top))
    def _():
        lat_ref[...] = jnp.where((place & 1) == 1, north_in[...], south)

    up.wait_send()
    pl.when(lat > 0)(down.wait_send)
    east.wait_send()
    west.wait_send()
    for t in tell:
        t.wait_send()


def halos(relays, plan, state, mask):
    fields, levels, rows, lanes = state.shape
    bands = lax.axis_size("lat")
    pack = (rows // 2, lanes)
    edge = (fields * levels, lanes)
    near = pl.BlockSpec(memory_space=pltpu.VMEM)
    anywhere = pl.BlockSpec(memory_space=pl.ANY)
    scalars = pl.BlockSpec(memory_space=pltpu.SMEM)
    return pl.pallas_call(
        functools.partial(halo_kernel, relays),
        in_specs=[scalars, anywhere, anywhere],
        out_specs=[near, near, near, scalars],
        out_shape=[
            jax.ShapeDtypeStruct(pack, F32),
            jax.ShapeDtypeStruct(edge, F32),
            jax.ShapeDtypeStruct(edge, F32),
            jax.ShapeDtypeStruct((1,), jnp.int32),
        ],
        scratch_shapes=[
            pltpu.VMEM(state.shape, F32),
            pltpu.VMEM(mask.shape, jnp.int32),
            pltpu.VMEM(pack, F32),
            pltpu.VMEM((2,) + edge, F32),
            pltpu.VMEM(pack, F32),
            pltpu.VMEM(pack, F32),
            pltpu.VMEM(edge, F32),
            pltpu.VMEM(edge, F32),
            pltpu.VMEM((8, lanes), jnp.int32),
            pltpu.VMEM((bands - 1, 8, lanes), jnp.int32),
            pltpu.SemaphoreType.DMA((fields + 1,)),
            pltpu.SemaphoreType.DMA((4 + bands - 1,)),
            pltpu.SemaphoreType.DMA((4 + bands - 1,)),
        ],
        compiler_params=pltpu.CompilerParams(
            collective_id=0, has_side_effects=True, vmem_limit_bytes=16 * MIB
        ),
    )(plan, state, mask)


def leaves(plan_ref, chips, chip, t, way):
    target = plan_ref[4 * chip + t] // 4
    return target == lax.rem(chip + way + chips, chips)


def pick(index, values):
    chosen = values[0]
    for at, value in enumerate(values[1:], 1):
        chosen = jnp.where(index == at, value, chosen)
    return chosen


def move_kernel(
    rounds,
    idle,
    plan_ref,
    state_ref,
    diff_ref,
    mask_ref,
    lat_ref,
    west_ref,
    east_ref,
    out_ref,
    padded,
    wet,
    mine,
    theirs,
    other,
    other_theirs,
    leaving,
    arrived,
    swapped,
    relayed,
    result,
    load_sem,
    store_sem,
    half_send,
    half_recv,
    tile_send,
    tile_recv,
    swap_send,
    swap_recv,
    leg_send,
    leg_recv,
    relay_send,
    relay_recv,
):
    fields, levels, rows, lanes = state_ref.shape
    planes = fields * levels
    quarter = rows // 4
    chunks = quarter // STEP
    devices, bands = lax.axis_size("lon"), lax.axis_size("lat")
    chips = devices // 2
    tiles = 4 * chips
    lon, lat = lax.axis_index("lon"), lax.axis_index("lat")
    chip, core = lon // 2, lax.rem(lon, 2)
    twin = {"lon": lon + 1 - 2 * core}
    ahead_lon = lax.rem(lon + 2, devices)
    behind_lon = lax.rem(lon + devices - 2, devices)
    ways = ((1, ahead_lon), (-1, behind_lon))
    keys = [(side, r) for side in range(2) for r in range(rounds)]
    active = None if idle is None else lat != idle

    def busy(work):
        if idle is None:
            work()
        else:
            pl.when(active)(work)

    def resting(work):
        if idle is not None:
            pl.when(lat == idle)(work)

    loads = [
        pltpu.make_async_copy(state_ref.at[f], padded.at[f, :, pl.ds(8, rows), :], load_sem.at[f])
        for f in range(fields)
    ]
    barrier = pltpu.get_barrier_semaphore()

    def greet(who):
        pl.semaphore_signal(barrier, inc=1, device_id=who, device_id_type=MESH)

    greet(twin)

    @busy
    def _():
        greet({"lon": ahead_lon})
        greet({"lon": behind_lon})
        if idle is not None:
            for at in (lon, ahead_lon, behind_lon):
                greet({"lat": idle, "lon": at})

    @resting
    def _():
        for o in range(1, bands):
            for at in (lon, ahead_lon, behind_lon):
                greet({"lat": (idle + o) % bands, "lon": at})

    for load in loads:
        load.start()

    wet[pl.ds(8, rows), :] = mask_ref[...].astype(F32)
    wet[0:8, :] = jnp.ones((8, lanes), F32)
    wet[rows + 8 : rows + 16, :] = jnp.ones((8, lanes), F32)
    for f in range(fields):
        for k in range(levels):
            i = f * levels + k
            padded[f, k, 7:8, :] = west_ref[i : i + 1, :]
            padded[f, k, rows + 8 : rows + 9, :] = east_ref[i : i + 1, :]

    chosen = {}
    for side, (way, _) in enumerate(ways):
        hits = [leaves(plan_ref, chips, chip, t, way) for t in range(4)]
        for r in range(rounds):
            count, tile = jnp.int32(0), jnp.int32(0)
            for t in range(4):
                tile = jnp.where(hits[t] & (count == r), t, tile)
                count = count + hits[t].astype(jnp.int32)
            chosen[side, r] = jnp.where(tile // 2 == core, 0, 2) + lax.rem(tile, 2)

    lane = lax.broadcasted_iota(jnp.int32, (STEP, lanes), 1)
    is_last = lane == lanes - 1
    is_first = lane == 0
    force = gradient_coef * weight_coef

    def solve(c, half, to_ref):
        def group(slot, _):
            row = pl.multiple_of(half * quarter + c * STEP, STEP)
            base = pl.multiple_of(slot * (2 * quarter) + row, STEP)
            edges = pltpu.roll(lat_ref[pl.ds(row, STEP), :], 64 * slot, 1)
            wet_c = wet[pl.ds(base + 8, STEP), :]
            wet_e = wet[pl.ds(base + 9, STEP), :]
            wet_w = wet[pl.ds(base + 7, STEP), :]
            zonal = meridional = None
            upper = []
            rhs = []
            for k in range(levels):
                center = [padded[f, k, pl.ds(base + 8, STEP), :] * wet_c for f in range(fields)]
                u, v = center[2], center[3]
                grad_x, grad_y, value = [], [], []
                for f in range(fields):
                    i = f * levels + k
                    e = padded[f, k, pl.ds(base + 9, STEP), :] * wet_e
                    w = padded[f, k, pl.ds(base + 7, STEP), :] * wet_w
                    edge = pltpu.roll(edges, (lanes - 2 - 2 * i) % lanes, 1)
                    n = jnp.where(is_last, edge, pltpu.roll(center[f], lanes - 1, 1))
                    s = jnp.where(is_first, edge, pltpu.roll(center[f], 1, 1))
                    gx, gy = e - w, n - s
                    grad_x.append(gx)
                    grad_y.append(gy)
                    total = (e + w) + (n + s)
                    flow = u * gx + v * gy
                    value.append(
                        (1.0 - 4.0 * diffuse_coef) * center[f] + (diffuse_coef * total - advect_coef * flow)
                    )
                dx = (force * haline_coef) * grad_x[1] - (force * thermal_coef) * grad_x[0]
                dy = (force * haline_coef) * grad_y[1] - (force * thermal_coef) * grad_y[0]
                zonal = dx if k == 0 else zonal + dx
                meridional = dy if k == 0 else meridional + dy
                value[2] = value[2] - zonal
                value[3] = value[3] - meridional
                lower_k = diff_ref[k - 1, pl.ds(base, STEP), :] if k > 0 else None
                upper_k = diff_ref[k, pl.ds(base, STEP), :] if k < levels - 1 else None
                pivot = 1.0
                if k > 0:
                    pivot = pivot + lower_k
                if k < levels - 1:
                    pivot = pivot + upper_k
                if k > 0:
                    pivot = pivot - lower_k * upper[k - 1]
                inverse = 1.0 / pivot
                upper.append(upper_k * inverse if k < levels - 1 else None)
                if k > 0:
                    value = [value[f] + lower_k * rhs[k - 1][f] for f in range(fields)]
                rhs.append([value[f] * inverse for f in range(fields)])
            for f in range(fields):
                x = rhs[levels - 1][f]
                to_ref[c, slot, f * levels + levels - 1] = x * wet_c
                for k in range(levels - 2, -1, -1):
                    x = rhs[k][f] + upper[k] * x
                    to_ref[c, slot, f * levels + k] = x * wet_c
            return 0

        lax.fori_loop(0, 2, group, 0)

    def first(c):
        return remote_copy(theirs.at[c], other.at[c], half_send.at[c, 0], half_recv.at[c, 0], twin)

    def second(c):
        return remote_copy(mine.at[c], other_theirs.at[c], half_send.at[c, 1], half_recv.at[c, 1], twin)

    def direct(c, side, r, part):
        return remote_copy(
            leaving.at[side, r, c, part],
            arrived.at[side, r, c, part],
            tile_send.at[c, side, r],
            tile_recv.at[c, side, r],
            {"lon": ways[side][1]},
        )

    def swap(c, side, r):
        return remote_copy(
            arrived.at[side, r, c],
            swapped.at[side, r, c],
            swap_send.at[c, side, r],
            swap_recv.at[c, side, r],
            twin,
        )

    relay_chunks = chunks // 2
    relays = RELAYED * relay_chunks - 1

    def part_of(n):
        return n // RELAYED, pl.ds(lax.rem(n, RELAYED) * levels, levels)

    def detour(side, n):
        j = lax.rem(lat - (idle + 1) + 2 * bands, bands)
        c, part = part_of(n)
        return remote_copy(
            leaving.at[side, 0, c, part],
            relayed.at[j, side, n],
            leg_send.at[side, n],
            leg_recv.at[j, side, n],
            {"lat": idle, "lon": ways[side][1]},
        )

    def forward(j, side, n):
        c, part = part_of(n)
        return remote_copy(
            relayed.at[j, side, n],
            arrived.at[side, 0, c, part],
            relay_send.at[j, side, n],
            relay_recv.at[side, n],
            {"lat": lax.rem(idle + 1 + j, bands)},
        )

    def pass_on(t):
        groups = []
        if idle is not None:
            above, below = list(range(bands - 1, idle, -1)), list(range(idle))
            while above or below:
                groups.append([rows.pop(0) for rows in (above, below) if rows])
        before, j, n = 0, jnp.int32(0), jnp.int32(0)
        for group in groups:
            at = t - before
            inside = at >= 0
            which = [(row - idle - 1) % bands for row in group]
            j = jnp.where(inside, pick(lax.rem(jnp.maximum(at, 0), len(group)), which), j)
            n = jnp.where(inside, jnp.maximum(at, 0) // len(group), n)
            before += relays * len(group)
        for side in range(2):
            here(j, side, n).wait_recv()
            forward(j, side, n).start()

    def here(j, side, n):
        return remote_copy(
            relayed.at[j, side, n], relayed.at[j, side, n], relay_send.at[j, side, n], leg_recv.at[j, side, n], twin
        )

    def each_part(c, work):
        if idle is None:
            work(slice(0, planes))
            return
        pl.when(c < relay_chunks - 1)(lambda: work(pl.ds(RELAYED * levels, planes - RELAYED * levels)))
        pl.when(c == relay_chunks - 1)(
            lambda: work(pl.ds((RELAYED - 1) * levels, planes - (RELAYED - 1) * levels))
        )
        pl.when(c >= relay_chunks)(lambda: work(slice(0, planes)))

    def each_relay(c, work):
        if idle is None:
            return
        for f in range(RELAYED):
            n = c * RELAYED + f
            pl.when(n < relays)(functools.partial(work, n))

    for load in loads:
        load.wait()

    def advance(c, _):
        solve(c, 1 - core, theirs)

        @pl.when(c == 0)
        def _():
            if idle is None:
                pl.semaphore_wait(barrier, 3)
            else:
                busy(lambda: pl.semaphore_wait(barrier, 6))
                resting(lambda: pl.semaphore_wait(barrier, 1 + 3 * (bands - 1)))

        first(c).start()
        solve(c, core, mine)

        @busy
        def _():
            first(c).wait_recv()

            def pack(i, _):
                held = [ref[c, slot, i] for ref in (mine, other) for slot in range(2)]
                for (side, r), index in chosen.items():
                    leaving[side, r, c, i] = pick(index, held)
                return 0

            lax.fori_loop(0, planes, pack, 0, unroll=8)
            def relay(n):
                for side in range(2):
                    detour(side, n).start()

            def send(part):
                for side, r in keys:
                    direct(c, side, r, part).start()

            each_relay(c, relay)
            each_part(c, send)

        second(c).start()

        @resting
        def _():
            @pl.when(c > 0)
            def _():
                pass_on(c - 1)

        return 0

    lax.fori_loop(0, chunks, advance, 0)

    origin = []
    for slot in range(2):
        target = 2 * lon + slot
        source = jnp.int32(0)
        for shift in range(-3, 4):
            g = lax.rem(target + shift + tiles, tiles)
            source = jnp.where(plan_ref[g] == target, g, source)
        from_chip, t = source // 4, lax.rem(source, 4)
        at = jnp.where(t // 2 == core, 0, 2) + lax.rem(t, 2)
        for side, (way, _) in enumerate(ways):
            came = from_chip == lax.rem(chip - way + chips, chips)
            rank = jnp.int32(0)
            for q in range(3):
                hit = leaves(plan_ref, chips, from_chip, q, way) & (q < t)
                rank = rank + hit.astype(jnp.int32)
            at = jnp.where(came, 4 + side * rounds + jnp.minimum(rank, rounds - 1), at)
        origin.append(at)

    def store(c, slot, part):
        half = core if part == 0 else 1 - core
        row = pl.multiple_of(2 * quarter * slot + half * quarter + c * STEP, STEP)
        return pltpu.make_async_copy(
            result.at[c, slot, part], out_ref.at[:, :, pl.ds(row, STEP), :], store_sem.at[c, slot, part]
        )

    def place(c):
        second(c).wait_recv()
        resting(first(c).wait_recv)

        @busy
        def _():
            for key in keys:
                swap(c, *key).wait_recv()

        def level(k, _):
            for f in range(fields):
                i = f * levels + k
                for part in range(2):
                    near, far, came = (
                        (mine, other, arrived) if part == 0 else (theirs, other_theirs, swapped)
                    )
                    values = [ref[c, slot, i] for ref in (near, far) for slot in range(2)]
                    values += [came[side, r, c, i] for side, r in keys]
                    for slot in range(2):
                        result[c, slot, part, f, k] = pick(origin[slot], values)
            return 0

        lax.fori_loop(0, levels, level, 0)
        for slot in range(2):
            for part in range(2):
                store(c, slot, part).start()

    def chunk_at(step):
        if idle is None:
            return step
        return step // 2 + relay_chunks * lax.rem(step, 2)

    left = (bands - 1) * relays - (chunks - 1)
    each_step = -(-left // chunks)

    def drain(step, _):
        @busy
        def _():
            @pl.when(step < chunks)
            def _():
                c = chunk_at(step)

                def receive(part):
                    for key in keys:
                        direct(c, *key, part).wait_recv()

                def receive_relay(n):
                    for side in range(2):
                        forward(0, side, n).wait_recv()

                each_part(c, receive)
                each_relay(c, receive_relay)
                for key in keys:
                    swap(c, *key).start()

        @resting
        def _():
            for more in range(each_step):
                t = step * each_step + more
                pl.when(t < left)(lambda: pass_on(chunks - 1 + t))

        @pl.when(step > 0)
        def _():
            place(chunk_at(step - 1))

        return 0

    lax.fori_loop(0, chunks + 1, drain, 0)

    def finish(c, _):
        first(c).wait_send()
        second(c).wait_send()

        @busy
        def _():
            def sent(part):
                for key in keys:
                    direct(c, *key, part).wait_send()

            def sent_relay(n):
                for side in range(2):
                    detour(side, n).wait_send()

            each_part(c, sent)
            each_relay(c, sent_relay)
            for key in keys:
                swap(c, *key).wait_send()

        for slot in range(2):
            for part in range(2):
                store(c, slot, part).wait()
        return 0

    lax.fori_loop(0, chunks, finish, 0)

    @resting
    def _():
        def relay_sent(n, _):
            for side in range(2):
                for j in range(bands - 1):
                    forward(j, side, n).wait_send()
            return 0

        lax.fori_loop(0, relays, relay_sent, 0)


def move(rounds, idle, plan, state, diffusivity, mask, lat_edges, west, east):
    fields, levels, rows, lanes = state.shape
    bands = lax.axis_size("lat")
    chunks = rows // 4 // STEP
    planes = fields * levels
    relays = RELAYED * (chunks // 2) - 1 if idle is not None else 1
    others = bands - 1 if idle is not None else 1
    anywhere = pl.BlockSpec(memory_space=pl.ANY)
    near = pl.BlockSpec(memory_space=pltpu.VMEM)
    halves = pltpu.VMEM((chunks, 2, planes, STEP, lanes), F32)
    pieces = pltpu.VMEM((2, rounds, chunks, planes, STEP, lanes), F32)
    dma = pltpu.SemaphoreType.DMA
    number = rounds if idle is None else 4 + idle
    return pl.pallas_call(
        functools.partial(move_kernel, rounds, idle),
        in_specs=[pl.BlockSpec(memory_space=pltpu.SMEM), anywhere] + [near] * 5,
        out_specs=anywhere,
        out_shape=jax.ShapeDtypeStruct(state.shape, F32),
        scratch_shapes=[
            pltpu.VMEM((fields, levels, rows + 16, lanes), F32),
            pltpu.VMEM((rows + 16, lanes), F32),
            halves,
            halves,
            halves,
            halves,
            pieces,
            pieces,
            pieces,
            pltpu.VMEM((others, 2, relays, levels, STEP, lanes), F32),
            pltpu.VMEM((chunks, 2, 2, fields, levels, STEP, lanes), F32),
            dma((fields,)),
            dma((chunks, 2, 2)),
            dma((chunks, 2)),
            dma((chunks, 2)),
            dma((chunks, 2, rounds)),
            dma((chunks, 2, rounds)),
            dma((chunks, 2, rounds)),
            dma((chunks, 2, rounds)),
            dma((2, relays)),
            dma((others, 2, relays)),
            dma((others, 2, relays)),
            dma((2, relays)),
        ],
        compiler_params=pltpu.CompilerParams(
            collective_id=number, has_side_effects=True, vmem_limit_bytes=(24 + 6 * rounds) * MIB
        ),
    )(plan, state, diffusivity, mask, lat_edges, west, east)


def local(relays, state, diffusivity, mask, tile_plan):
    plan = tile_plan.reshape(-1)
    lat_edges, west, east, branch = halos(relays, plan, state, mask)
    branches = [functools.partial(move, rounds, None) for rounds in (1, 2, 3)]
    if relays:
        branches = [functools.partial(move, 1, row) for row in range(lax.axis_size("lat"))] + branches
    return lax.switch(branch[0], branches, plan, state, diffusivity, mask, lat_edges, west, east)


def solution(mesh):
    placed = (P(None, None, "lon", "lat"), P(None, "lon", "lat"), P("lon", "lat"), P(None, "lat"))
    relays = mesh.shape["lat"] == 4
    return jax.shard_map(
        functools.partial(local, relays),
        mesh=mesh,
        in_specs=placed,
        out_specs=P(None, None, "lon", "lat"),
        check_vma=False,
    )
```

```python
import functools

import jax
import jax.numpy as jnp
from jax import lax
from jax.experimental import pallas as pl
from jax.experimental.pallas import tpu as pltpu
from jax.sharding import PartitionSpec as P

advect_coef = 0.1
diffuse_coef = 0.1
gradient_coef = 0.1
thermal_coef = 0.2
haline_coef = 0.15
weight_coef = 0.25

F32 = jnp.float32
MIB = 1 << 20
MESH = pl.DeviceIdType.MESH
STEP = 8
RELAYS = 7
RELAYED = 2


def remote_copy(source, target, send, recv, who):
    return pltpu.make_async_remote_copy(
        src_ref=source, dst_ref=target, send_sem=send, recv_sem=recv, device_id=who, device_id_type=MESH
    )


def halo_kernel(
    relays,
    plan_ref,
    state_ref,
    mask_ref,
    diff_ref,
    lat_ref,
    padded,
    wet,
    diff_out,
    branch_ref,
    mask,
    lat_pack,
    lon_pack,
    north_in,
    south_in,
    west_in,
    east_in,
    count,
    counts_in,
    load_sem,
    send_sem,
    recv_sem,
):
    fields, levels, rows, lanes = state_ref.shape
    half, quarter = rows // 2, rows // 4
    pairs = fields // 2
    width = lanes // 4
    lane = lax.broadcasted_iota(jnp.int32, (8, lanes), 1)
    devices, bands = lax.axis_size("lon"), lax.axis_size("lat")
    lon, lat = lax.axis_index("lon"), lax.axis_index("lat")
    top = lat == bands - 1
    to_east = {"lon": lax.rem(lon + 1, devices)}
    to_west = {"lon": lax.rem(lon + devices - 1, devices)}
    across = {"lon": devices - 1 - lon}
    others = [{"lat": lax.rem(lat + o, bands)} for o in range(1, bands)]
    barrier = pltpu.get_barrier_semaphore()
    for who in [to_east, to_west, across] + others:
        pl.semaphore_signal(barrier, inc=1, device_id=who, device_id_type=MESH)

    mask_load = pltpu.make_async_copy(mask_ref, mask, load_sem.at[fields])
    mask_load.start()
    loads = [
        pltpu.make_async_copy(state_ref.at[f], padded.at[f, :, pl.ds(8, rows), :], load_sem.at[f])
        for f in range(fields)
    ]
    for load in loads:
        load.start()
    diff_load = pltpu.make_async_copy(diff_ref, diff_out, load_sem.at[fields + 1])
    diff_load.start()

    chips = devices // 2

    def leaving(chip, most):
        for way in (1, -1):
            number = jnp.int32(0)
            for t in range(4):
                number = number + leaves(plan_ref, chips, chip, t, way).astype(jnp.int32)
            most = jnp.maximum(most, number)
        return most

    most = lax.fori_loop(0, chips, leaving, jnp.int32(0))
    count[...] = jnp.full(count.shape, most, jnp.int32)

    def remote(source, target, at, recv_at, who):
        return remote_copy(source, target, send_sem.at[at], recv_sem.at[recv_at], who)

    north_who, south_who = {"lat": jnp.minimum(lat + 1, bands - 1)}, {"lat": jnp.maximum(lat - 1, 0)}
    up = [remote(lat_pack.at[q], south_in.at[q], q, q, north_who) for q in range(pairs)]
    down = [remote(lat_pack.at[q], north_in.at[q], pairs + q, pairs + q, south_who) for q in range(pairs)]
    fold = [remote(lat_pack.at[q], north_in.at[q], q, pairs + q, across) for q in range(pairs)]
    at_lon = 2 * pairs
    east = remote(lon_pack.at[1], west_in, at_lon, at_lon, to_east)
    west = remote(lon_pack.at[0], east_in, at_lon + 1, at_lon + 1, to_west)
    tell = [
        remote(count, counts_in.at[o], at_lon + 2 + o, at_lon + 2 + o, who) for o, who in enumerate(others)
    ]
    pl.semaphore_wait(barrier, 3 + bands - 1)
    for t in tell:
        t.start()
    mask_load.wait()
    wet[pl.ds(8, rows), :] = mask[...].astype(F32)
    wet[0:8, :] = jnp.ones((8, lanes), F32)
    wet[rows + 8 : rows + 16, :] = jnp.ones((8, lanes), F32)
    for q in range(pairs):
        pair = (2 * q, 2 * q + 1)
        for f in pair:
            loads[f].wait()

        def group(g, _):
            blocks = []
            for h in range(2):
                for slot in range(2):
                    at = pl.ds(pl.multiple_of(slot * half + h * quarter + g * 8 + 8, 8), 8)
                    cover = wet[at, :]
                    block = jnp.zeros((8, lanes), F32)
                    for f in pair:
                        for k in range(levels):
                            place = (2 * h + slot) * width + 2 * ((f - 2 * q) * levels + k)
                            x = pltpu.roll(padded[f, k, at, :] * cover, place + 1, 1)
                            block = jnp.where((lane >> 1) == (place >> 1), x, block)
                    blocks.append(block)
            to = pl.ds(pl.multiple_of(g * 8, 8), 8)
            lower = jnp.where(lane < width, blocks[0], blocks[1])
            upper = jnp.where(lane < 3 * width, blocks[2], blocks[3])
            lat_pack[q, to, :] = jnp.where(lane < 2 * width, lower, upper)
            return 0

        lax.fori_loop(0, quarter // 8, group, 0)
        pl.when(top)(fold[q].start)
        pl.when(jnp.logical_not(top))(up[q].start)
        pl.when(lat > 0)(down[q].start)

    first = wet[8:9, :]
    final = wet[rows + 7 : rows + 8, :]
    for f in range(fields):
        at_field = slice(f * levels, (f + 1) * levels)
        lon_pack[0, at_field, :] = jnp.concatenate([padded[f, k, 8:9, :] for k in range(levels)], 0) * first
        lon_pack[1, at_field, :] = (
            jnp.concatenate([padded[f, k, rows + 7 : rows + 8, :] for k in range(levels)], 0) * final
        )
    east.start()
    west.start()

    values = [count[...]]
    value_rows = [lat]
    for o, t in enumerate(tell):
        t.wait_recv()
        values.append(counts_in[o])
        value_rows.append(lax.rem(lat + bands - o - 1, bands))
    largest, idle = values[0], jnp.full(count.shape, bands, jnp.int32)
    for value, row in zip(values, value_rows):
        largest = jnp.maximum(largest, value)
        idle = jnp.minimum(idle, jnp.where(value == 0, row, bands))
    if relays:
        branch = jnp.where(largest <= 1, idle, bands - 1 + largest)
    else:
        branch = jnp.maximum(largest, 1) - 1
    branch_ref[0] = jnp.max(branch)
    east.wait_recv()
    west.wait_recv()
    for f in range(fields):
        for k in range(levels):
            i = f * levels + k
            padded[f, k, 7:8, :] = west_in[i : i + 1, :]
            padded[f, k, rows + 8 : rows + 9, :] = east_in[i : i + 1, :]

    @pl.when(lat > 0)
    def _():
        for copy in up:
            copy.wait_recv()

    @pl.when(lat == 0)
    def _():
        south_in[...] = jnp.zeros_like(south_in)

    for copy in down:
        copy.wait_recv()
    sub = lax.broadcasted_iota(jnp.int32, (8, lanes), 0)
    odd = (lane & 1) == 1
    outer = (lane // width) % 2 == 1
    groups = quarter // 8
    for q in range(pairs):
        sign = 1.0 if q == 0 else -1.0

        @pl.when(top)
        def _():
            for g in range(groups):
                x = north_in[q, (groups - 1 - g) * 8 : (groups - g) * 8, :]
                x = pltpu.roll(x, 4, 0)
                x = jnp.where((sub & 2) == 0, pltpu.roll(x, 6, 0), pltpu.roll(x, 2, 0))
                x = jnp.where((sub & 1) == 0, pltpu.roll(x, 7, 0), pltpu.roll(x, 1, 0))
                x = jnp.where(outer, pltpu.roll(x, 3 * width + 1, 1), pltpu.roll(x, width + 1, 1)) * sign
                south = pltpu.roll(south_in[q, g * 8 : g * 8 + 8, :], 2, 1)
                lat_ref[q, g * 8 : g * 8 + 8, :] = jnp.where(odd, x, south)

        @pl.when(jnp.logical_not(top))
        def _():
            for g in range(groups):
                south = pltpu.roll(south_in[q, g * 8 : g * 8 + 8, :], 2, 1)
                lat_ref[q, g * 8 : g * 8 + 8, :] = jnp.where(odd, north_in[q, g * 8 : g * 8 + 8, :], south)

    diff_load.wait()
    for q in range(pairs):
        up[q].wait_send()
        pl.when(lat > 0)(down[q].wait_send)
    east.wait_send()
    west.wait_send()
    for t in tell:
        t.wait_send()


def halos(relays, plan, state, mask, diffusivity):
    fields, levels, rows, lanes = state.shape
    bands = lax.axis_size("lat")
    pack = (fields // 2, rows // 4, lanes)
    edge = (fields * levels, lanes)
    near = pl.BlockSpec(memory_space=pltpu.VMEM)
    anywhere = pl.BlockSpec(memory_space=pl.ANY)
    scalars = pl.BlockSpec(memory_space=pltpu.SMEM)
    return pl.pallas_call(
        functools.partial(halo_kernel, relays),
        in_specs=[scalars, anywhere, anywhere, anywhere],
        out_specs=[near, near, near, near, scalars],
        out_shape=[
            jax.ShapeDtypeStruct(pack, F32),
            jax.ShapeDtypeStruct((fields, levels, rows + 16, lanes), F32),
            jax.ShapeDtypeStruct((rows + 16, lanes), F32),
            jax.ShapeDtypeStruct(diffusivity.shape, F32),
            jax.ShapeDtypeStruct((1,), jnp.int32),
        ],
        scratch_shapes=[
            pltpu.VMEM(mask.shape, jnp.int32),
            pltpu.VMEM(pack, F32),
            pltpu.VMEM((2,) + edge, F32),
            pltpu.VMEM(pack, F32),
            pltpu.VMEM(pack, F32),
            pltpu.VMEM(edge, F32),
            pltpu.VMEM(edge, F32),
            pltpu.VMEM((8, lanes), jnp.int32),
            pltpu.VMEM((bands - 1, 8, lanes), jnp.int32),
            pltpu.SemaphoreType.DMA((fields + 2,)),
            pltpu.SemaphoreType.DMA((fields + 2 + bands - 1,)),
            pltpu.SemaphoreType.DMA((fields + 2 + bands - 1,)),
        ],
        compiler_params=pltpu.CompilerParams(
            collective_id=0, has_side_effects=True, vmem_limit_bytes=55 * MIB
        ),
    )(plan, state, mask, diffusivity)


def leaves(plan_ref, chips, chip, t, way):
    target = plan_ref[4 * chip + t] // 4
    return target == lax.rem(chip + way + chips, chips)


def pick(index, values):
    chosen = values[0]
    for at, value in enumerate(values[1:], 1):
        chosen = jnp.where(index == at, value, chosen)
    return chosen


def move_kernel(
    rounds,
    idle,
    plan_ref,
    padded,
    wet,
    diff_ref,
    lat_ref,
    out_ref,
    mine,
    theirs,
    other,
    other_theirs,
    leaving,
    arrived,
    swapped,
    relayed,
    half_send,
    half_recv,
    tile_send,
    tile_recv,
    swap_send,
    swap_recv,
    leg_send,
    leg_recv,
    relay_send,
    relay_recv,
):
    fields, levels, rows, lanes = out_ref.shape
    planes = fields * levels
    quarter = rows // 4
    chunks = quarter // STEP
    devices, bands = lax.axis_size("lon"), lax.axis_size("lat")
    chips = devices // 2
    tiles = 4 * chips
    lon, lat = lax.axis_index("lon"), lax.axis_index("lat")
    chip, core = lon // 2, lax.rem(lon, 2)
    twin = {"lon": lon + 1 - 2 * core}
    ahead_lon = lax.rem(lon + 2, devices)
    behind_lon = lax.rem(lon + devices - 2, devices)
    ways = ((1, ahead_lon), (-1, behind_lon))
    keys = [(side, r) for side in range(2) for r in range(rounds)]
    active = None if idle is None else lat != idle

    def busy(work):
        if idle is None:
            work()
        else:
            pl.when(active)(work)

    def resting(work):
        if idle is not None:
            pl.when(lat == idle)(work)

    barrier = pltpu.get_barrier_semaphore()

    def greet(who):
        pl.semaphore_signal(barrier, inc=1, device_id=who, device_id_type=MESH)

    greet(twin)

    @busy
    def _():
        greet({"lon": ahead_lon})
        greet({"lon": behind_lon})
        if idle is not None:
            for at in (lon, ahead_lon, behind_lon):
                greet({"lat": idle, "lon": at})

    @resting
    def _():
        for o in range(1, bands):
            for at in (lon, ahead_lon, behind_lon):
                greet({"lat": (idle + o) % bands, "lon": at})

    chosen = {}
    for side, (way, _) in enumerate(ways):
        hits = [leaves(plan_ref, chips, chip, t, way) for t in range(4)]
        for r in range(rounds):
            count, tile = jnp.int32(0), jnp.int32(0)
            for t in range(4):
                tile = jnp.where(hits[t] & (count == r), t, tile)
                count = count + hits[t].astype(jnp.int32)
            chosen[side, r] = jnp.where(tile // 2 == core, 0, 2) + lax.rem(tile, 2)

    lane = lax.broadcasted_iota(jnp.int32, (STEP, lanes), 1)
    is_last = lane == lanes - 1
    is_first = lane == 0
    force = gradient_coef * weight_coef

    def solve(c, half, to_ref):
        def group(slot, _):
            row = pl.multiple_of(half * quarter + c * STEP, STEP)
            base = pl.multiple_of(slot * (2 * quarter) + row, STEP)
            turn = lax.rem(lanes - (2 * half + slot) * (lanes // 4), lanes)
            at = pl.ds(pl.multiple_of(c * STEP, STEP), STEP)
            edges = [pltpu.roll(lat_ref[q, at, :], turn, 1) for q in range(fields // 2)]
            wet_c = wet[pl.ds(base + 8, STEP), :]
            wet_e = wet[pl.ds(base + 9, STEP), :]
            wet_w = wet[pl.ds(base + 7, STEP), :]
            zonal = meridional = None
            upper = []
            rhs = []
            for k in range(levels):
                center = [padded[f, k, pl.ds(base + 8, STEP), :] * wet_c for f in range(fields)]
                u, v = center[2], center[3]
                grad_x, grad_y, value = [], [], []
                for f in range(fields):
                    e = padded[f, k, pl.ds(base + 9, STEP), :] * wet_e
                    w = padded[f, k, pl.ds(base + 7, STEP), :] * wet_w
                    edge = pltpu.roll(edges[f // 2], lanes - 2 - 2 * (f % 2 * levels + k), 1)
                    n = jnp.where(is_last, edge, pltpu.roll(center[f], lanes - 1, 1))
                    s = jnp.where(is_first, edge, pltpu.roll(center[f], 1, 1))
                    gx, gy = e - w, n - s
                    grad_x.append(gx)
                    grad_y.append(gy)
                    total = (e + w) + (n + s)
                    flow = u * gx + v * gy
                    value.append(
                        (1.0 - 4.0 * diffuse_coef) * center[f] + (diffuse_coef * total - advect_coef * flow)
                    )
                dx = (force * haline_coef) * grad_x[1] - (force * thermal_coef) * grad_x[0]
                dy = (force * haline_coef) * grad_y[1] - (force * thermal_coef) * grad_y[0]
                zonal = dx if k == 0 else zonal + dx
                meridional = dy if k == 0 else meridional + dy
                value[2] = value[2] - zonal
                value[3] = value[3] - meridional
                lower_k = diff_ref[k - 1, pl.ds(base, STEP), :] if k > 0 else None
                upper_k = diff_ref[k, pl.ds(base, STEP), :] if k < levels - 1 else None
                pivot = 1.0
                if k > 0:
                    pivot = pivot + lower_k
                if k < levels - 1:
                    pivot = pivot + upper_k
                if k > 0:
                    pivot = pivot - lower_k * upper[k - 1]
                inverse = 1.0 / pivot
                upper.append(upper_k * inverse if k < levels - 1 else None)
                if k > 0:
                    value = [value[f] + lower_k * rhs[k - 1][f] for f in range(fields)]
                rhs.append([value[f] * inverse for f in range(fields)])
            for f in range(fields):
                x = rhs[levels - 1][f]
                to_ref[c, slot, f * levels + levels - 1] = x * wet_c
                for k in range(levels - 2, -1, -1):
                    x = rhs[k][f] + upper[k] * x
                    to_ref[c, slot, f * levels + k] = x * wet_c
            return 0

        lax.fori_loop(0, 2, group, 0)

    def first(c):
        return remote_copy(theirs.at[c], other.at[c], half_send.at[c, 0], half_recv.at[c, 0], twin)

    def second(c):
        return remote_copy(mine.at[c], other_theirs.at[c], half_send.at[c, 1], half_recv.at[c, 1], twin)

    def direct(c, side, r, part):
        return remote_copy(
            leaving.at[side, r, c, part],
            arrived.at[side, r, c, part],
            tile_send.at[c, side, r],
            tile_recv.at[c, side, r],
            {"lon": ways[side][1]},
        )

    def swap(c, side, r):
        return remote_copy(
            arrived.at[side, r, c],
            swapped.at[side, r, c],
            swap_send.at[c, side, r],
            swap_recv.at[c, side, r],
            twin,
        )

    relay_chunks = chunks // 2
    relays = min(RELAYS, RELAYED * relay_chunks)

    def part_of(n):
        return n // RELAYED, pl.ds(lax.rem(n, RELAYED) * levels, levels)

    def detour(side, n):
        j = lax.rem(lat - (idle + 1) + 2 * bands, bands)
        c, part = part_of(n)
        return remote_copy(
            leaving.at[side, 0, c, part],
            relayed.at[j, side, n],
            leg_send.at[side, n],
            leg_recv.at[j, side, n],
            {"lat": idle, "lon": ways[side][1]},
        )

    def forward(j, side, n):
        c, part = part_of(n)
        return remote_copy(
            relayed.at[j, side, n],
            arrived.at[side, 0, c, part],
            relay_send.at[j, side, n],
            relay_recv.at[side, n],
            {"lat": lax.rem(idle + 1 + j, bands)},
        )

    def pass_on(t):
        groups = []
        if idle is not None:
            above, below = list(range(bands - 1, idle, -1)), list(range(idle))
            while above or below:
                groups.append([rows.pop(0) for rows in (above, below) if rows])
        before, j, n = 0, jnp.int32(0), jnp.int32(0)
        for group in groups:
            at = t - before
            inside = at >= 0
            which = [(row - idle - 1) % bands for row in group]
            j = jnp.where(inside, pick(lax.rem(jnp.maximum(at, 0), len(group)), which), j)
            n = jnp.where(inside, jnp.maximum(at, 0) // len(group), n)
            before += relays * len(group)
        for side in range(2):
            here(j, side, n).wait_recv()
            forward(j, side, n).start()

    def here(j, side, n):
        return remote_copy(
            relayed.at[j, side, n], relayed.at[j, side, n], relay_send.at[j, side, n], leg_recv.at[j, side, n], twin
        )

    def each_part(c, work):
        if idle is None:
            work(slice(0, planes))
            return
        for number in range(RELAYED + 1):
            skipped = number * levels
            around = jnp.clip(relays - c * RELAYED, 0, RELAYED) == number
            pl.when(around)(functools.partial(work, pl.ds(skipped, planes - skipped)))

    def each_relay(c, work):
        if idle is None:
            return
        for f in range(RELAYED):
            n = c * RELAYED + f
            pl.when(n < relays)(functools.partial(work, n))

    def advance(c, _):
        solve(c, 1 - core, theirs)

        @pl.when(c == 0)
        def _():
            if idle is None:
                pl.semaphore_wait(barrier, 3)
            else:
                busy(lambda: pl.semaphore_wait(barrier, 6))
                resting(lambda: pl.semaphore_wait(barrier, 1 + 3 * (bands - 1)))

        first(c).start()
        solve(c, core, mine)

        @busy
        def _():
            first(c).wait_recv()

            def pack(i, _):
                held = [ref[c, slot, i] for ref in (mine, other) for slot in range(2)]
                for (side, r), index in chosen.items():
                    leaving[side, r, c, i] = pick(index, held)
                return 0

            lax.fori_loop(0, planes, pack, 0, unroll=8)
            def relay(n):
                for side in range(2):
                    detour(side, n).start()

            def send(part):
                for side, r in keys:
                    direct(c, side, r, part).start()

            each_relay(c, relay)
            each_part(c, send)

        second(c).start()

        @resting
        def _():
            @pl.when((c > 0) & (c - 1 < (bands - 1) * relays))
            def _():
                pass_on(c - 1)

        return 0

    lax.fori_loop(0, chunks, advance, 0)

    origin = []
    for slot in range(2):
        target = 2 * lon + slot
        source = jnp.int32(0)
        for shift in range(-3, 4):
            g = lax.rem(target + shift + tiles, tiles)
            source = jnp.where(plan_ref[g] == target, g, source)
        from_chip, t = source // 4, lax.rem(source, 4)
        at = jnp.where(t // 2 == core, 0, 2) + lax.rem(t, 2)
        for side, (way, _) in enumerate(ways):
            came = from_chip == lax.rem(chip - way + chips, chips)
            rank = jnp.int32(0)
            for q in range(3):
                hit = leaves(plan_ref, chips, from_chip, q, way) & (q < t)
                rank = rank + hit.astype(jnp.int32)
            at = jnp.where(came, 4 + side * rounds + jnp.minimum(rank, rounds - 1), at)
        origin.append(at)

    def place(c):
        second(c).wait_recv()
        resting(first(c).wait_recv)

        @busy
        def _():
            for key in keys:
                swap(c, *key).wait_recv()

        def level(k, _):
            for f in range(fields):
                i = f * levels + k
                for part in range(2):
                    near, far, came = (
                        (mine, other, arrived) if part == 0 else (theirs, other_theirs, swapped)
                    )
                    values = [ref[c, slot, i] for ref in (near, far) for slot in range(2)]
                    values += [came[side, r, c, i] for side, r in keys]
                    half = core if part == 0 else 1 - core
                    for slot in range(2):
                        row = pl.multiple_of(2 * quarter * slot + half * quarter + c * STEP, STEP)
                        out_ref[f, k, pl.ds(row, STEP), :] = pick(origin[slot], values)
            return 0

        lax.fori_loop(0, levels, level, 0)

    def chunk_at(step):
        if idle is None:
            return step
        return step // 2 + relay_chunks * lax.rem(step, 2)

    def finish(c):
        first(c).wait_send()
        second(c).wait_send()

        @busy
        def _():
            def sent(part):
                for key in keys:
                    direct(c, *key, part).wait_send()

            def sent_relay(n):
                for side in range(2):
                    detour(side, n).wait_send()

            each_part(c, sent)
            each_relay(c, sent_relay)
            for key in keys:
                swap(c, *key).wait_send()

    left = (bands - 1) * relays - (chunks - 1)
    each_step = -(-left // chunks)

    def drain(step, _):
        @busy
        def _():
            @pl.when(step < chunks)
            def _():
                c = chunk_at(step)

                def receive(part):
                    for key in keys:
                        direct(c, *key, part).wait_recv()

                def receive_relay(n):
                    for side in range(2):
                        forward(0, side, n).wait_recv()

                each_part(c, receive)
                each_relay(c, receive_relay)
                for key in keys:
                    swap(c, *key).start()

        @resting
        def _():
            for more in range(each_step):
                t = step * each_step + more
                pl.when(t < left)(lambda: pass_on(chunks - 1 + t))

        @pl.when(step > 0)
        def _():
            place(chunk_at(step - 1))
            finish(chunk_at(step - 1))

        return 0

    lax.fori_loop(0, chunks + 1, drain, 0)

    @resting
    def _():
        def relay_sent(n, _):
            for side in range(2):
                for j in range(bands - 1):
                    forward(j, side, n).wait_send()
            return 0

        lax.fori_loop(0, relays, relay_sent, 0)


def move(rounds, idle, plan, padded, wet, diffusivity, lat_edges):
    fields, levels, rows, lanes = padded.shape
    rows = rows - 16
    bands = lax.axis_size("lat")
    chunks = rows // 4 // STEP
    planes = fields * levels
    relays = min(RELAYS, RELAYED * (chunks // 2)) if idle is not None else 1
    others = bands - 1 if idle is not None else 1
    near = pl.BlockSpec(memory_space=pltpu.VMEM)
    halves = pltpu.VMEM((chunks, 2, planes, STEP, lanes), F32)
    pieces = pltpu.VMEM((2, rounds, chunks, planes, STEP, lanes), F32)
    dma = pltpu.SemaphoreType.DMA
    number = rounds if idle is None else 4 + idle
    return pl.pallas_call(
        functools.partial(move_kernel, rounds, idle),
        in_specs=[pl.BlockSpec(memory_space=pltpu.SMEM), near, near, near, near],
        out_specs=near,
        out_shape=jax.ShapeDtypeStruct((fields, levels, rows, lanes), F32),
        scratch_shapes=[
            halves,
            halves,
            halves,
            halves,
            pieces,
            pieces,
            pieces,
            pltpu.VMEM((others, 2, relays, levels, STEP, lanes), F32),
            dma((chunks, 2)),
            dma((chunks, 2)),
            dma((chunks, 2, rounds)),
            dma((chunks, 2, rounds)),
            dma((chunks, 2, rounds)),
            dma((chunks, 2, rounds)),
            dma((2, relays)),
            dma((others, 2, relays)),
            dma((others, 2, relays)),
            dma((2, relays)),
        ],
        compiler_params=pltpu.CompilerParams(
            collective_id=number, has_side_effects=True, vmem_limit_bytes=(24 + 6 * rounds) * MIB
        ),
    )(plan, padded, wet, diffusivity, lat_edges)


def local(relays, state, diffusivity, mask, tile_plan):
    plan = tile_plan.reshape(-1)
    lat_edges, padded, wet, diff, branch = halos(relays, plan, state, mask, diffusivity)
    branches = [functools.partial(move, rounds, None) for rounds in (1, 2, 3)]
    if relays:
        branches = [functools.partial(move, 1, row) for row in range(lax.axis_size("lat"))] + branches
    return lax.switch(branch[0], branches, plan, padded, wet, diff, lat_edges)


def solution(mesh):
    placed = (P(None, None, "lon", "lat"), P(None, "lon", "lat"), P("lon", "lat"), P(None, "lat"))
    relays = mesh.shape["lat"] == 4
    return jax.shard_map(
        functools.partial(local, relays),
        mesh=mesh,
        in_specs=placed,
        out_specs=P(None, None, "lon", "lat"),
        check_vma=False,
    )
```

```python
import functools

import jax
import jax.numpy as jnp
from jax import lax
from jax.experimental import pallas as pl
from jax.experimental.pallas import tpu as pltpu
from jax.sharding import PartitionSpec as P

advect_coef = 0.1
diffuse_coef = 0.1
gradient_coef = 0.1
thermal_coef = 0.2
haline_coef = 0.15
weight_coef = 0.25

F32 = jnp.float32
MIB = 1 << 20
MESH = pl.DeviceIdType.MESH
STEP = 8
RELAYED = 2


def relay_plan(idle, bands):
    busy = [row for row in range(bands) if row not in idle]
    if len(idle) == 1:
        row = idle[0]
        above, below = list(range(bands - 1, row, -1)), list(range(row))
        groups = []
        while above or below:
            groups.append([side.pop(0) for side in (above, below) if side])
        return {row: groups}, 7
    if idle[1] < busy[0] or busy[1] < idle[0]:
        return {idle[0]: [[busy[1]]], idle[1]: [[busy[0]]]}, 10
    return {idle[0]: [[busy[0]]], idle[1]: [[busy[1]]]}, 14


def idle_sets(bands):
    single = [(row,) for row in range(bands)]
    return single + [(a, b) for a in range(bands) for b in range(a + 1, bands)]


def remote_copy(source, target, send, recv, who):
    return pltpu.make_async_remote_copy(
        src_ref=source, dst_ref=target, send_sem=send, recv_sem=recv, device_id=who, device_id_type=MESH
    )


def halo_kernel(
    relays,
    plan_ref,
    state_ref,
    mask_ref,
    diff_ref,
    lat_ref,
    padded,
    wet,
    diff_out,
    branch_ref,
    mask,
    lat_pack,
    lon_pack,
    north_in,
    south_in,
    west_in,
    east_in,
    count,
    counts_in,
    load_sem,
    send_sem,
    recv_sem,
):
    fields, levels, rows, lanes = state_ref.shape
    half, quarter = rows // 2, rows // 4
    pairs = fields // 2
    width = lanes // 4
    lane = lax.broadcasted_iota(jnp.int32, (8, lanes), 1)
    devices, bands = lax.axis_size("lon"), lax.axis_size("lat")
    lon, lat = lax.axis_index("lon"), lax.axis_index("lat")
    top = lat == bands - 1
    to_east = {"lon": lax.rem(lon + 1, devices)}
    to_west = {"lon": lax.rem(lon + devices - 1, devices)}
    across = {"lon": devices - 1 - lon}
    others = [{"lat": lax.rem(lat + o, bands)} for o in range(1, bands)]
    barrier = pltpu.get_barrier_semaphore()
    for who in [to_east, to_west, across] + others:
        pl.semaphore_signal(barrier, inc=1, device_id=who, device_id_type=MESH)

    mask_load = pltpu.make_async_copy(mask_ref, mask, load_sem.at[fields])
    mask_load.start()
    loads = [
        pltpu.make_async_copy(state_ref.at[f], padded.at[f, :, pl.ds(8, rows), :], load_sem.at[f])
        for f in range(fields)
    ]
    for load in loads:
        load.start()
    diff_load = pltpu.make_async_copy(diff_ref, diff_out, load_sem.at[fields + 1])
    diff_load.start()

    chips = devices // 2

    def leaving(chip, most):
        for way in (1, -1):
            number = jnp.int32(0)
            for t in range(4):
                number = number + leaves(plan_ref, chips, chip, t, way).astype(jnp.int32)
            most = jnp.maximum(most, number)
        return most

    most = lax.fori_loop(0, chips, leaving, jnp.int32(0))
    count[...] = jnp.full(count.shape, most, jnp.int32)

    def remote(source, target, at, recv_at, who):
        return remote_copy(source, target, send_sem.at[at], recv_sem.at[recv_at], who)

    north_who, south_who = {"lat": jnp.minimum(lat + 1, bands - 1)}, {"lat": jnp.maximum(lat - 1, 0)}
    up = [remote(lat_pack.at[q], south_in.at[q], q, q, north_who) for q in range(pairs)]
    down = [remote(lat_pack.at[q], north_in.at[q], pairs + q, pairs + q, south_who) for q in range(pairs)]
    fold = [remote(lat_pack.at[q], north_in.at[q], q, pairs + q, across) for q in range(pairs)]
    at_lon = 2 * pairs
    east = remote(lon_pack.at[1], west_in, at_lon, at_lon, to_east)
    west = remote(lon_pack.at[0], east_in, at_lon + 1, at_lon + 1, to_west)
    tell = [
        remote(count, counts_in.at[o], at_lon + 2 + o, at_lon + 2 + o, who) for o, who in enumerate(others)
    ]
    pl.semaphore_wait(barrier, 3 + bands - 1)
    for t in tell:
        t.start()
    mask_load.wait()
    wet[pl.ds(8, rows), :] = mask[...].astype(F32)
    wet[0:8, :] = jnp.ones((8, lanes), F32)
    wet[rows + 8 : rows + 16, :] = jnp.ones((8, lanes), F32)
    for q in range(pairs):
        pair = (2 * q, 2 * q + 1)
        for f in pair:
            loads[f].wait()

        def group(g, _):
            blocks = []
            for h in range(2):
                for slot in range(2):
                    at = pl.ds(pl.multiple_of(slot * half + h * quarter + g * 8 + 8, 8), 8)
                    cover = wet[at, :]
                    block = jnp.zeros((8, lanes), F32)
                    for f in pair:
                        for k in range(levels):
                            place = (2 * h + slot) * width + 2 * ((f - 2 * q) * levels + k)
                            x = pltpu.roll(padded[f, k, at, :] * cover, place + 1, 1)
                            block = jnp.where((lane >> 1) == (place >> 1), x, block)
                    blocks.append(block)
            to = pl.ds(pl.multiple_of(g * 8, 8), 8)
            lower = jnp.where(lane < width, blocks[0], blocks[1])
            upper = jnp.where(lane < 3 * width, blocks[2], blocks[3])
            lat_pack[q, to, :] = jnp.where(lane < 2 * width, lower, upper)
            return 0

        lax.fori_loop(0, quarter // 8, group, 0)
        pl.when(top)(fold[q].start)
        pl.when(jnp.logical_not(top))(up[q].start)
        pl.when(lat > 0)(down[q].start)

    first = wet[8:9, :]
    final = wet[rows + 7 : rows + 8, :]
    for f in range(fields):
        at_field = slice(f * levels, (f + 1) * levels)
        lon_pack[0, at_field, :] = jnp.concatenate([padded[f, k, 8:9, :] for k in range(levels)], 0) * first
        lon_pack[1, at_field, :] = (
            jnp.concatenate([padded[f, k, rows + 7 : rows + 8, :] for k in range(levels)], 0) * final
        )
    east.start()
    west.start()

    values = [count[...]]
    value_rows = [lat]
    for o, t in enumerate(tell):
        t.wait_recv()
        values.append(counts_in[o])
        value_rows.append(lax.rem(lat + bands - o - 1, bands))
    largest = values[0]
    for value in values[1:]:
        largest = jnp.maximum(largest, value)
    branch = jnp.maximum(largest, 1) - 1
    if relays:
        sets = idle_sets(bands)
        branch = branch + len(sets)
        rests = []
        for row in range(bands):
            at_rest = jnp.zeros(count.shape, jnp.int32)
            for value, value_row in zip(values, value_rows):
                at_rest = jnp.where((value == 0) & (value_row == row), 1, at_rest)
            rests.append(at_rest == 1)
        for number, rows_at_rest in enumerate(sets):
            all_rest = functools.reduce(jnp.logical_and, [rests[row] for row in rows_at_rest])
            branch = jnp.where(all_rest & (largest <= 1), number, branch)
    branch_ref[0] = jnp.max(branch)
    east.wait_recv()
    west.wait_recv()
    for f in range(fields):
        for k in range(levels):
            i = f * levels + k
            padded[f, k, 7:8, :] = west_in[i : i + 1, :]
            padded[f, k, rows + 8 : rows + 9, :] = east_in[i : i + 1, :]

    @pl.when(lat > 0)
    def _():
        for copy in up:
            copy.wait_recv()

    @pl.when(lat == 0)
    def _():
        south_in[...] = jnp.zeros_like(south_in)

    for copy in down:
        copy.wait_recv()
    sub = lax.broadcasted_iota(jnp.int32, (8, lanes), 0)
    odd = (lane & 1) == 1
    outer = (lane // width) % 2 == 1
    groups = quarter // 8
    for q in range(pairs):
        sign = 1.0 if q == 0 else -1.0

        @pl.when(top)
        def _():
            for g in range(groups):
                x = north_in[q, (groups - 1 - g) * 8 : (groups - g) * 8, :]
                x = pltpu.roll(x, 4, 0)
                x = jnp.where((sub & 2) == 0, pltpu.roll(x, 6, 0), pltpu.roll(x, 2, 0))
                x = jnp.where((sub & 1) == 0, pltpu.roll(x, 7, 0), pltpu.roll(x, 1, 0))
                x = jnp.where(outer, pltpu.roll(x, 3 * width + 1, 1), pltpu.roll(x, width + 1, 1)) * sign
                south = pltpu.roll(south_in[q, g * 8 : g * 8 + 8, :], 2, 1)
                lat_ref[q, g * 8 : g * 8 + 8, :] = jnp.where(odd, x, south)

        @pl.when(jnp.logical_not(top))
        def _():
            for g in range(groups):
                south = pltpu.roll(south_in[q, g * 8 : g * 8 + 8, :], 2, 1)
                lat_ref[q, g * 8 : g * 8 + 8, :] = jnp.where(odd, north_in[q, g * 8 : g * 8 + 8, :], south)

    diff_load.wait()
    for q in range(pairs):
        up[q].wait_send()
        pl.when(lat > 0)(down[q].wait_send)
    east.wait_send()
    west.wait_send()
    for t in tell:
        t.wait_send()


def halos(relays, plan, state, mask, diffusivity):
    fields, levels, rows, lanes = state.shape
    bands = lax.axis_size("lat")
    pack = (fields // 2, rows // 4, lanes)
    edge = (fields * levels, lanes)
    near = pl.BlockSpec(memory_space=pltpu.VMEM)
    anywhere = pl.BlockSpec(memory_space=pl.ANY)
    scalars = pl.BlockSpec(memory_space=pltpu.SMEM)
    return pl.pallas_call(
        functools.partial(halo_kernel, relays),
        in_specs=[scalars, anywhere, anywhere, anywhere],
        out_specs=[near, near, near, near, scalars],
        out_shape=[
            jax.ShapeDtypeStruct(pack, F32),
            jax.ShapeDtypeStruct((fields, levels, rows + 16, lanes), F32),
            jax.ShapeDtypeStruct((rows + 16, lanes), F32),
            jax.ShapeDtypeStruct(diffusivity.shape, F32),
            jax.ShapeDtypeStruct((1,), jnp.int32),
        ],
        scratch_shapes=[
            pltpu.VMEM(mask.shape, jnp.int32),
            pltpu.VMEM(pack, F32),
            pltpu.VMEM((2,) + edge, F32),
            pltpu.VMEM(pack, F32),
            pltpu.VMEM(pack, F32),
            pltpu.VMEM(edge, F32),
            pltpu.VMEM(edge, F32),
            pltpu.VMEM((8, lanes), jnp.int32),
            pltpu.VMEM((bands - 1, 8, lanes), jnp.int32),
            pltpu.SemaphoreType.DMA((fields + 2,)),
            pltpu.SemaphoreType.DMA((fields + 2 + bands - 1,)),
            pltpu.SemaphoreType.DMA((fields + 2 + bands - 1,)),
        ],
        compiler_params=pltpu.CompilerParams(
            collective_id=0, has_side_effects=True, vmem_limit_bytes=55 * MIB
        ),
    )(plan, state, mask, diffusivity)


def leaves(plan_ref, chips, chip, t, way):
    target = plan_ref[4 * chip + t] // 4
    return target == lax.rem(chip + way + chips, chips)


def pick(index, values):
    chosen = values[0]
    for at, value in enumerate(values[1:], 1):
        chosen = jnp.where(index == at, value, chosen)
    return chosen


def move_kernel(
    rounds,
    idle,
    plan_ref,
    padded,
    wet,
    diff_ref,
    lat_ref,
    out_ref,
    mine,
    theirs,
    other,
    other_theirs,
    leaving,
    arrived,
    swapped,
    relayed,
    half_send,
    half_recv,
    tile_send,
    tile_recv,
    swap_send,
    swap_recv,
    leg_send,
    leg_recv,
    relay_send,
    relay_recv,
):
    fields, levels, rows, lanes = out_ref.shape
    planes = fields * levels
    quarter = rows // 4
    chunks = quarter // STEP
    devices, bands = lax.axis_size("lon"), lax.axis_size("lat")
    chips = devices // 2
    tiles = 4 * chips
    lon, lat = lax.axis_index("lon"), lax.axis_index("lat")
    chip, core = lon // 2, lax.rem(lon, 2)
    twin = {"lon": lon + 1 - 2 * core}
    ahead_lon = lax.rem(lon + 2, devices)
    behind_lon = lax.rem(lon + devices - 2, devices)
    ways = ((1, ahead_lon), (-1, behind_lon))
    keys = [(side, r) for side in range(2) for r in range(rounds)]
    if idle is None:
        served, relays, active, resting_now = {}, 0, None, None
    else:
        served, relays = relay_plan(idle, bands)
        resting_now = functools.reduce(jnp.logical_or, [lat == row for row in idle])
        active = jnp.logical_not(resting_now)
        order = {row: sum(groups, []) for row, groups in served.items()}
        others = len(order[idle[0]])
        relay_row, relay_at = jnp.int32(0), jnp.int32(0)
        for row, rows_served in order.items():
            for j, busy_row in enumerate(rows_served):
                relay_row = jnp.where(lat == busy_row, row, relay_row)
                relay_at = jnp.where(lat == busy_row, j, relay_at)

    def served_row(j):
        row = jnp.int32(0)
        for at, rows_served in order.items():
            row = jnp.where(lat == at, pick(j, rows_served), row)
        return row

    def busy(work):
        if idle is None:
            work()
        else:
            pl.when(active)(work)

    def resting(work):
        if idle is not None:
            pl.when(resting_now)(work)

    barrier = pltpu.get_barrier_semaphore()

    def greet(who):
        pl.semaphore_signal(barrier, inc=1, device_id=who, device_id_type=MESH)

    greet(twin)

    @busy
    def _():
        greet({"lon": ahead_lon})
        greet({"lon": behind_lon})
        if idle is not None:
            for at in (lon, ahead_lon, behind_lon):
                greet({"lat": relay_row, "lon": at})

    @resting
    def _():
        for j in range(others):
            for at in (lon, ahead_lon, behind_lon):
                greet({"lat": served_row(j), "lon": at})

    chosen = {}
    for side, (way, _) in enumerate(ways):
        hits = [leaves(plan_ref, chips, chip, t, way) for t in range(4)]
        for r in range(rounds):
            count, tile = jnp.int32(0), jnp.int32(0)
            for t in range(4):
                tile = jnp.where(hits[t] & (count == r), t, tile)
                count = count + hits[t].astype(jnp.int32)
            chosen[side, r] = jnp.where(tile // 2 == core, 0, 2) + lax.rem(tile, 2)

    lane = lax.broadcasted_iota(jnp.int32, (STEP, lanes), 1)
    is_last = lane == lanes - 1
    is_first = lane == 0
    force = gradient_coef * weight_coef

    def solve(c, half, to_ref):
        def group(slot, _):
            row = pl.multiple_of(half * quarter + c * STEP, STEP)
            base = pl.multiple_of(slot * (2 * quarter) + row, STEP)
            turn = lax.rem(lanes - (2 * half + slot) * (lanes // 4), lanes)
            at = pl.ds(pl.multiple_of(c * STEP, STEP), STEP)
            edges = [pltpu.roll(lat_ref[q, at, :], turn, 1) for q in range(fields // 2)]
            wet_c = wet[pl.ds(base + 8, STEP), :]
            wet_e = wet[pl.ds(base + 9, STEP), :]
            wet_w = wet[pl.ds(base + 7, STEP), :]
            zonal = meridional = None
            upper = []
            rhs = []
            for k in range(levels):
                center = [padded[f, k, pl.ds(base + 8, STEP), :] * wet_c for f in range(fields)]
                u, v = center[2], center[3]
                grad_x, grad_y, value = [], [], []
                for f in range(fields):
                    e = padded[f, k, pl.ds(base + 9, STEP), :] * wet_e
                    w = padded[f, k, pl.ds(base + 7, STEP), :] * wet_w
                    edge = pltpu.roll(edges[f // 2], lanes - 2 - 2 * (f % 2 * levels + k), 1)
                    n = jnp.where(is_last, edge, pltpu.roll(center[f], lanes - 1, 1))
                    s = jnp.where(is_first, edge, pltpu.roll(center[f], 1, 1))
                    gx, gy = e - w, n - s
                    grad_x.append(gx)
                    grad_y.append(gy)
                    total = (e + w) + (n + s)
                    flow = u * gx + v * gy
                    value.append(
                        (1.0 - 4.0 * diffuse_coef) * center[f] + (diffuse_coef * total - advect_coef * flow)
                    )
                dx = (force * haline_coef) * grad_x[1] - (force * thermal_coef) * grad_x[0]
                dy = (force * haline_coef) * grad_y[1] - (force * thermal_coef) * grad_y[0]
                zonal = dx if k == 0 else zonal + dx
                meridional = dy if k == 0 else meridional + dy
                value[2] = value[2] - zonal
                value[3] = value[3] - meridional
                lower_k = diff_ref[k - 1, pl.ds(base, STEP), :] if k > 0 else None
                upper_k = diff_ref[k, pl.ds(base, STEP), :] if k < levels - 1 else None
                pivot = 1.0
                if k > 0:
                    pivot = pivot + lower_k
                if k < levels - 1:
                    pivot = pivot + upper_k
                if k > 0:
                    pivot = pivot - lower_k * upper[k - 1]
                inverse = 1.0 / pivot
                upper.append(upper_k * inverse if k < levels - 1 else None)
                if k > 0:
                    value = [value[f] + lower_k * rhs[k - 1][f] for f in range(fields)]
                rhs.append([value[f] * inverse for f in range(fields)])
            for f in range(fields):
                x = rhs[levels - 1][f]
                to_ref[c, slot, f * levels + levels - 1] = x * wet_c
                for k in range(levels - 2, -1, -1):
                    x = rhs[k][f] + upper[k] * x
                    to_ref[c, slot, f * levels + k] = x * wet_c
            return 0

        lax.fori_loop(0, 2, group, 0)

    def first(c):
        return remote_copy(theirs.at[c], other.at[c], half_send.at[c, 0], half_recv.at[c, 0], twin)

    def second(c):
        return remote_copy(mine.at[c], other_theirs.at[c], half_send.at[c, 1], half_recv.at[c, 1], twin)

    def direct(c, side, r, part):
        return remote_copy(
            leaving.at[side, r, c, part],
            arrived.at[side, r, c, part],
            tile_send.at[c, side, r],
            tile_recv.at[c, side, r],
            {"lon": ways[side][1]},
        )

    def swap(c, side, r):
        return remote_copy(
            arrived.at[side, r, c],
            swapped.at[side, r, c],
            swap_send.at[c, side, r],
            swap_recv.at[c, side, r],
            twin,
        )


    def part_of(n):
        return n // RELAYED, pl.ds(lax.rem(n, RELAYED) * levels, levels)

    def detour(side, n):
        j = relay_at
        c, part = part_of(n)
        return remote_copy(
            leaving.at[side, 0, c, part],
            relayed.at[j, side, n],
            leg_send.at[side, n],
            leg_recv.at[j, side, n],
            {"lat": relay_row, "lon": ways[side][1]},
        )

    def forward(j, side, n):
        c, part = part_of(n)
        return remote_copy(
            relayed.at[j, side, n],
            arrived.at[side, 0, c, part],
            relay_send.at[j, side, n],
            relay_recv.at[side, n],
            {"lat": served_row(j)},
        )

    def pass_on(t):
        groups = [len(group) for group in served[idle[0]]]
        before, j, n = 0, jnp.int32(0), jnp.int32(0)
        for number, size in enumerate(groups):
            at = jnp.maximum(t - before * relays, 0)
            inside = t >= before * relays
            j = jnp.where(inside, before + lax.rem(at, size), j)
            n = jnp.where(inside, at // size, n)
            before += size
        for side in range(2):
            here(j, side, n).wait_recv()
            forward(j, side, n).start()

    def here(j, side, n):
        return remote_copy(
            relayed.at[j, side, n], relayed.at[j, side, n], relay_send.at[j, side, n], leg_recv.at[j, side, n], twin
        )

    def each_part(c, work):
        if idle is None:
            work(slice(0, planes))
            return
        for number in range(RELAYED + 1):
            skipped = number * levels
            around = jnp.clip(relays - c * RELAYED, 0, RELAYED) == number
            pl.when(around)(functools.partial(work, pl.ds(skipped, planes - skipped)))

    def each_relay(c, work):
        if idle is None:
            return
        for f in range(RELAYED):
            n = c * RELAYED + f
            pl.when(n < relays)(functools.partial(work, n))

    def advance(c, _):
        solve(c, 1 - core, theirs)

        @pl.when(c == 0)
        def _():
            if idle is None:
                pl.semaphore_wait(barrier, 3)
            else:
                busy(lambda: pl.semaphore_wait(barrier, 6))
                resting(lambda: pl.semaphore_wait(barrier, 1 + 3 * others))

        first(c).start()
        solve(c, core, mine)

        @busy
        def _():
            first(c).wait_recv()

            def pack(i, _):
                held = [ref[c, slot, i] for ref in (mine, other) for slot in range(2)]
                for (side, r), index in chosen.items():
                    leaving[side, r, c, i] = pick(index, held)
                return 0

            lax.fori_loop(0, planes, pack, 0, unroll=8)
            def relay(n):
                for side in range(2):
                    detour(side, n).start()

            def send(part):
                for side, r in keys:
                    direct(c, side, r, part).start()

            each_relay(c, relay)
            each_part(c, send)

        second(c).start()

        @resting
        def _():
            @pl.when((c > 0) & (c - 1 < others * relays))
            def _():
                pass_on(c - 1)

        return 0

    lax.fori_loop(0, chunks, advance, 0)

    origin = []
    for slot in range(2):
        target = 2 * lon + slot
        source = jnp.int32(0)
        for shift in range(-3, 4):
            g = lax.rem(target + shift + tiles, tiles)
            source = jnp.where(plan_ref[g] == target, g, source)
        from_chip, t = source // 4, lax.rem(source, 4)
        at = jnp.where(t // 2 == core, 0, 2) + lax.rem(t, 2)
        for side, (way, _) in enumerate(ways):
            came = from_chip == lax.rem(chip - way + chips, chips)
            rank = jnp.int32(0)
            for q in range(3):
                hit = leaves(plan_ref, chips, from_chip, q, way) & (q < t)
                rank = rank + hit.astype(jnp.int32)
            at = jnp.where(came, 4 + side * rounds + jnp.minimum(rank, rounds - 1), at)
        origin.append(at)

    def place(c):
        second(c).wait_recv()
        resting(first(c).wait_recv)

        @busy
        def _():
            for key in keys:
                swap(c, *key).wait_recv()

        def level(k, _):
            for f in range(fields):
                i = f * levels + k
                for part in range(2):
                    near, far, came = (
                        (mine, other, arrived) if part == 0 else (theirs, other_theirs, swapped)
                    )
                    values = [ref[c, slot, i] for ref in (near, far) for slot in range(2)]
                    values += [came[side, r, c, i] for side, r in keys]
                    half = core if part == 0 else 1 - core
                    for slot in range(2):
                        row = pl.multiple_of(2 * quarter * slot + half * quarter + c * STEP, STEP)
                        out_ref[f, k, pl.ds(row, STEP), :] = pick(origin[slot], values)
            return 0

        lax.fori_loop(0, levels, level, 0)

    def chunk_at(step):
        if idle is None:
            return step
        arrival, sent = [], 0
        for c in range(chunks):
            around = min(max(relays - c * RELAYED, 0), RELAYED)
            sent += fields - around
            arrival.append([sent, (c * RELAYED + around) if around else 0])
        arrival = [max(here / sent, there / relays) for here, there in arrival]
        return pick(step, sorted(range(chunks), key=lambda c: arrival[c]))

    def finish(c):
        first(c).wait_send()
        second(c).wait_send()

        @busy
        def _():
            def sent(part):
                for key in keys:
                    direct(c, *key, part).wait_send()

            def sent_relay(n):
                for side in range(2):
                    detour(side, n).wait_send()

            each_part(c, sent)
            each_relay(c, sent_relay)
            for key in keys:
                swap(c, *key).wait_send()

    left = others * relays - (chunks - 1) if idle is not None else 0
    each_step = -(-left // chunks)

    def drain(step, _):
        @busy
        def _():
            @pl.when(step < chunks)
            def _():
                c = chunk_at(step)

                def receive(part):
                    for key in keys:
                        direct(c, *key, part).wait_recv()

                def receive_relay(n):
                    for side in range(2):
                        forward(0, side, n).wait_recv()

                each_part(c, receive)
                each_relay(c, receive_relay)
                for key in keys:
                    swap(c, *key).start()

        @resting
        def _():
            for more in range(each_step):
                t = step * each_step + more
                pl.when(t < left)(lambda: pass_on(chunks - 1 + t))

        @pl.when(step > 0)
        def _():
            place(chunk_at(step - 1))
            finish(chunk_at(step - 1))

        return 0

    lax.fori_loop(0, chunks + 1, drain, 0)

    @resting
    def _():
        def relay_sent(n, _):
            for side in range(2):
                for j in range(others):
                    forward(j, side, n).wait_send()
            return 0

        lax.fori_loop(0, relays, relay_sent, 0)


def move(rounds, idle, plan, padded, wet, diffusivity, lat_edges):
    fields, levels, rows, lanes = padded.shape
    rows = rows - 16
    bands = lax.axis_size("lat")
    chunks = rows // 4 // STEP
    planes = fields * levels
    others, relays = 1, 1
    if idle is not None:
        served, relays = relay_plan(idle, bands)
        others = sum(len(group) for group in served[idle[0]])
    near = pl.BlockSpec(memory_space=pltpu.VMEM)
    halves = pltpu.VMEM((chunks, 2, planes, STEP, lanes), F32)
    pieces = pltpu.VMEM((2, rounds, chunks, planes, STEP, lanes), F32)
    dma = pltpu.SemaphoreType.DMA
    number = rounds if idle is None else 4 + idle_sets(bands).index(idle)
    return pl.pallas_call(
        functools.partial(move_kernel, rounds, idle),
        in_specs=[pl.BlockSpec(memory_space=pltpu.SMEM), near, near, near, near],
        out_specs=near,
        out_shape=jax.ShapeDtypeStruct((fields, levels, rows, lanes), F32),
        scratch_shapes=[
            halves,
            halves,
            halves,
            halves,
            pieces,
            pieces,
            pieces,
            pltpu.VMEM((others, 2, relays, levels, STEP, lanes), F32),
            dma((chunks, 2)),
            dma((chunks, 2)),
            dma((chunks, 2, rounds)),
            dma((chunks, 2, rounds)),
            dma((chunks, 2, rounds)),
            dma((chunks, 2, rounds)),
            dma((2, relays)),
            dma((others, 2, relays)),
            dma((others, 2, relays)),
            dma((2, relays)),
        ],
        compiler_params=pltpu.CompilerParams(
            collective_id=number, has_side_effects=True, vmem_limit_bytes=(24 + 6 * rounds) * MIB
        ),
    )(plan, padded, wet, diffusivity, lat_edges)


def local(relays, state, diffusivity, mask, tile_plan):
    plan = tile_plan.reshape(-1)
    lat_edges, padded, wet, diff, branch = halos(relays, plan, state, mask, diffusivity)
    branches = [functools.partial(move, rounds, None) for rounds in (1, 2, 3)]
    if relays:
        branches = [functools.partial(move, 1, idle) for idle in idle_sets(lax.axis_size("lat"))] + branches
    return lax.switch(branch[0], branches, plan, padded, wet, diff, lat_edges)


def solution(mesh):
    placed = (P(None, None, "lon", "lat"), P(None, "lon", "lat"), P("lon", "lat"), P(None, "lat"))
    relays = mesh.shape["lat"] == 4
    return jax.shard_map(
        functools.partial(local, relays),
        mesh=mesh,
        in_specs=placed,
        out_specs=P(None, None, "lon", "lat"),
        check_vma=False,
    )
```

```python
import functools

import jax
import jax.numpy as jnp
from jax import lax
from jax.experimental import pallas as pl
from jax.experimental.pallas import tpu as pltpu
from jax.sharding import PartitionSpec as P

advect_coef = 0.1
diffuse_coef = 0.1
gradient_coef = 0.1
thermal_coef = 0.2
haline_coef = 0.15
weight_coef = 0.25

F32 = jnp.float32
MIB = 1 << 20
MESH = pl.DeviceIdType.MESH
STEP = 8
RELAYED = 2


def relay_plan(idle, bands):
    busy = [row for row in range(bands) if row not in idle]
    if len(idle) == 1:
        row = idle[0]
        above, below = list(range(bands - 1, row, -1)), list(range(row))
        groups = []
        while above or below:
            groups.append([side.pop(0) for side in (above, below) if side])
        return {row: groups}, 7
    if idle[1] < busy[0] or busy[1] < idle[0]:
        return {idle[0]: [[busy[1]]], idle[1]: [[busy[0]]]}, 10
    return {idle[0]: [[busy[0]]], idle[1]: [[busy[1]]]}, 15


def idle_sets(bands):
    single = [(row,) for row in range(bands)]
    return single + [(a, b) for a in range(bands) for b in range(a + 1, bands)]


def remote_copy(source, target, send, recv, who):
    return pltpu.make_async_remote_copy(
        src_ref=source, dst_ref=target, send_sem=send, recv_sem=recv, device_id=who, device_id_type=MESH
    )


def halo_kernel(
    relays,
    plan_ref,
    state_ref,
    mask_ref,
    diff_ref,
    lat_ref,
    padded,
    wet,
    diff_out,
    branch_ref,
    mask,
    lat_pack,
    lon_pack,
    north_in,
    south_in,
    west_in,
    east_in,
    count,
    counts_in,
    load_sem,
    send_sem,
    recv_sem,
):
    fields, levels, rows, lanes = state_ref.shape
    half, quarter = rows // 2, rows // 4
    pairs = fields // 2
    width = lanes // 4
    lane = lax.broadcasted_iota(jnp.int32, (8, lanes), 1)
    devices, bands = lax.axis_size("lon"), lax.axis_size("lat")
    lon, lat = lax.axis_index("lon"), lax.axis_index("lat")
    top = lat == bands - 1
    to_east = {"lon": lax.rem(lon + 1, devices)}
    to_west = {"lon": lax.rem(lon + devices - 1, devices)}
    across = {"lon": devices - 1 - lon}
    others = [{"lat": lax.rem(lat + o, bands)} for o in range(1, bands)]
    barrier = pltpu.get_barrier_semaphore()
    for who in [to_east, to_west, across] + others:
        pl.semaphore_signal(barrier, inc=1, device_id=who, device_id_type=MESH)

    mask_load = pltpu.make_async_copy(mask_ref, mask, load_sem.at[fields])
    mask_load.start()
    loads = [
        pltpu.make_async_copy(state_ref.at[f], padded.at[f, :, pl.ds(8, rows), :], load_sem.at[f])
        for f in range(fields)
    ]
    for load in loads:
        load.start()
    diff_load = pltpu.make_async_copy(diff_ref, diff_out, load_sem.at[fields + 1])
    diff_load.start()

    chips = devices // 2

    def leaving(chip, most):
        for way in (1, -1):
            number = jnp.int32(0)
            for t in range(4):
                number = number + leaves(plan_ref, chips, chip, t, way).astype(jnp.int32)
            most = jnp.maximum(most, number)
        return most

    most = lax.fori_loop(0, chips, leaving, jnp.int32(0))
    count[...] = jnp.full(count.shape, most, jnp.int32)

    def remote(source, target, at, recv_at, who):
        return remote_copy(source, target, send_sem.at[at], recv_sem.at[recv_at], who)

    north_who, south_who = {"lat": jnp.minimum(lat + 1, bands - 1)}, {"lat": jnp.maximum(lat - 1, 0)}
    up = [remote(lat_pack.at[q], south_in.at[q], q, q, north_who) for q in range(pairs)]
    down = [remote(lat_pack.at[q], north_in.at[q], pairs + q, pairs + q, south_who) for q in range(pairs)]
    fold = [remote(lat_pack.at[q], north_in.at[q], q, pairs + q, across) for q in range(pairs)]
    at_lon = 2 * pairs
    east = remote(lon_pack.at[1], west_in, at_lon, at_lon, to_east)
    west = remote(lon_pack.at[0], east_in, at_lon + 1, at_lon + 1, to_west)
    tell = [
        remote(count, counts_in.at[o], at_lon + 2 + o, at_lon + 2 + o, who) for o, who in enumerate(others)
    ]
    pl.semaphore_wait(barrier, 3 + bands - 1)
    for t in tell:
        t.start()
    mask_load.wait()
    wet[pl.ds(8, rows), :] = mask[...].astype(F32)
    wet[0:8, :] = jnp.ones((8, lanes), F32)
    wet[rows + 8 : rows + 16, :] = jnp.ones((8, lanes), F32)
    for q in range(pairs):
        pair = (2 * q, 2 * q + 1)
        for f in pair:
            loads[f].wait()

        def group(g, _):
            blocks = []
            for h in range(2):
                for slot in range(2):
                    at = pl.ds(pl.multiple_of(slot * half + h * quarter + g * 8 + 8, 8), 8)
                    cover = wet[at, :]
                    block = jnp.zeros((8, lanes), F32)
                    for f in pair:
                        for k in range(levels):
                            place = (2 * h + slot) * width + 2 * ((f - 2 * q) * levels + k)
                            x = pltpu.roll(padded[f, k, at, :] * cover, place + 1, 1)
                            block = jnp.where((lane >> 1) == (place >> 1), x, block)
                    blocks.append(block)
            to = pl.ds(pl.multiple_of(g * 8, 8), 8)
            lower = jnp.where(lane < width, blocks[0], blocks[1])
            upper = jnp.where(lane < 3 * width, blocks[2], blocks[3])
            lat_pack[q, to, :] = jnp.where(lane < 2 * width, lower, upper)
            return 0

        lax.fori_loop(0, quarter // 8, group, 0, unroll=2)
        pl.when(top)(fold[q].start)
        pl.when(jnp.logical_not(top))(up[q].start)
        pl.when(lat > 0)(down[q].start)

    first = wet[8:9, :]
    final = wet[rows + 7 : rows + 8, :]
    for f in range(fields):
        at_field = slice(f * levels, (f + 1) * levels)
        lon_pack[0, at_field, :] = jnp.concatenate([padded[f, k, 8:9, :] for k in range(levels)], 0) * first
        lon_pack[1, at_field, :] = (
            jnp.concatenate([padded[f, k, rows + 7 : rows + 8, :] for k in range(levels)], 0) * final
        )
    east.start()
    west.start()

    values = [count[...]]
    value_rows = [lat]
    for o, t in enumerate(tell):
        t.wait_recv()
        values.append(counts_in[o])
        value_rows.append(lax.rem(lat + bands - o - 1, bands))
    largest = values[0]
    for value in values[1:]:
        largest = jnp.maximum(largest, value)
    branch = jnp.maximum(largest, 1) - 1
    if relays:
        sets = idle_sets(bands)
        branch = branch + len(sets)
        rests = []
        for row in range(bands):
            at_rest = jnp.zeros(count.shape, jnp.int32)
            for value, value_row in zip(values, value_rows):
                at_rest = jnp.where((value == 0) & (value_row == row), 1, at_rest)
            rests.append(at_rest == 1)
        for number, rows_at_rest in enumerate(sets):
            all_rest = functools.reduce(jnp.logical_and, [rests[row] for row in rows_at_rest])
            branch = jnp.where(all_rest & (largest <= 1), number, branch)
    branch_ref[0] = jnp.max(branch)
    east.wait_recv()
    west.wait_recv()
    for f in range(fields):
        for k in range(levels):
            i = f * levels + k
            padded[f, k, 7:8, :] = west_in[i : i + 1, :]
            padded[f, k, rows + 8 : rows + 9, :] = east_in[i : i + 1, :]

    @pl.when(lat > 0)
    def _():
        for copy in up:
            copy.wait_recv()

    @pl.when(lat == 0)
    def _():
        south_in[...] = jnp.zeros_like(south_in)

    for copy in down:
        copy.wait_recv()
    sub = lax.broadcasted_iota(jnp.int32, (8, lanes), 0)
    odd = (lane & 1) == 1
    outer = (lane // width) % 2 == 1
    groups = quarter // 8
    for q in range(pairs):
        sign = 1.0 if q == 0 else -1.0

        @pl.when(top)
        def _():
            for g in range(groups):
                x = north_in[q, (groups - 1 - g) * 8 : (groups - g) * 8, :]
                x = pltpu.roll(x, 4, 0)
                x = jnp.where((sub & 2) == 0, pltpu.roll(x, 6, 0), pltpu.roll(x, 2, 0))
                x = jnp.where((sub & 1) == 0, pltpu.roll(x, 7, 0), pltpu.roll(x, 1, 0))
                x = jnp.where(outer, pltpu.roll(x, 3 * width + 1, 1), pltpu.roll(x, width + 1, 1)) * sign
                south = pltpu.roll(south_in[q, g * 8 : g * 8 + 8, :], 2, 1)
                lat_ref[q, g * 8 : g * 8 + 8, :] = jnp.where(odd, x, south)

        @pl.when(jnp.logical_not(top))
        def _():
            for g in range(groups):
                south = pltpu.roll(south_in[q, g * 8 : g * 8 + 8, :], 2, 1)
                lat_ref[q, g * 8 : g * 8 + 8, :] = jnp.where(odd, north_in[q, g * 8 : g * 8 + 8, :], south)

    diff_load.wait()
    for q in range(pairs):
        up[q].wait_send()
        pl.when(lat > 0)(down[q].wait_send)
    east.wait_send()
    west.wait_send()
    for t in tell:
        t.wait_send()


def halos(relays, plan, state, mask, diffusivity):
    fields, levels, rows, lanes = state.shape
    bands = lax.axis_size("lat")
    pack = (fields // 2, rows // 4, lanes)
    edge = (fields * levels, lanes)
    near = pl.BlockSpec(memory_space=pltpu.VMEM)
    anywhere = pl.BlockSpec(memory_space=pl.ANY)
    scalars = pl.BlockSpec(memory_space=pltpu.SMEM)
    return pl.pallas_call(
        functools.partial(halo_kernel, relays),
        in_specs=[scalars, anywhere, anywhere, anywhere],
        out_specs=[near, near, near, near, scalars],
        out_shape=[
            jax.ShapeDtypeStruct(pack, F32),
            jax.ShapeDtypeStruct((fields, levels, rows + 16, lanes), F32),
            jax.ShapeDtypeStruct((rows + 16, lanes), F32),
            jax.ShapeDtypeStruct(diffusivity.shape, F32),
            jax.ShapeDtypeStruct((1,), jnp.int32),
        ],
        scratch_shapes=[
            pltpu.VMEM(mask.shape, jnp.int32),
            pltpu.VMEM(pack, F32),
            pltpu.VMEM((2,) + edge, F32),
            pltpu.VMEM(pack, F32),
            pltpu.VMEM(pack, F32),
            pltpu.VMEM(edge, F32),
            pltpu.VMEM(edge, F32),
            pltpu.VMEM((8, lanes), jnp.int32),
            pltpu.VMEM((bands - 1, 8, lanes), jnp.int32),
            pltpu.SemaphoreType.DMA((fields + 2,)),
            pltpu.SemaphoreType.DMA((fields + 2 + bands - 1,)),
            pltpu.SemaphoreType.DMA((fields + 2 + bands - 1,)),
        ],
        compiler_params=pltpu.CompilerParams(
            collective_id=0, has_side_effects=True, vmem_limit_bytes=55 * MIB
        ),
    )(plan, state, mask, diffusivity)


def leaves(plan_ref, chips, chip, t, way):
    target = plan_ref[4 * chip + t] // 4
    return target == lax.rem(chip + way + chips, chips)


def pick(index, values):
    chosen = values[0]
    for at, value in enumerate(values[1:], 1):
        chosen = jnp.where(index == at, value, chosen)
    return chosen


def move_kernel(
    rounds,
    idle,
    plan_ref,
    padded,
    wet,
    diff_ref,
    lat_ref,
    out_ref,
    mine,
    theirs,
    other,
    other_theirs,
    leaving,
    arrived,
    swapped,
    relayed,
    half_send,
    half_recv,
    tile_send,
    tile_recv,
    swap_send,
    swap_recv,
    leg_send,
    leg_recv,
    relay_send,
    relay_recv,
):
    fields, levels, rows, lanes = out_ref.shape
    planes = fields * levels
    quarter = rows // 4
    chunks = quarter // STEP
    devices, bands = lax.axis_size("lon"), lax.axis_size("lat")
    chips = devices // 2
    tiles = 4 * chips
    lon, lat = lax.axis_index("lon"), lax.axis_index("lat")
    chip, core = lon // 2, lax.rem(lon, 2)
    twin = {"lon": lon + 1 - 2 * core}
    ahead_lon = lax.rem(lon + 2, devices)
    behind_lon = lax.rem(lon + devices - 2, devices)
    ways = ((1, ahead_lon), (-1, behind_lon))
    keys = [(side, r) for side in range(2) for r in range(rounds)]
    if idle is None:
        served, relays, active, resting_now = {}, 0, None, None
    else:
        served, relays = relay_plan(idle, bands)
        resting_now = functools.reduce(jnp.logical_or, [lat == row for row in idle])
        active = jnp.logical_not(resting_now)
        order = {row: sum(groups, []) for row, groups in served.items()}
        others = len(order[idle[0]])
        relay_row, relay_at = jnp.int32(0), jnp.int32(0)
        for row, rows_served in order.items():
            for j, busy_row in enumerate(rows_served):
                relay_row = jnp.where(lat == busy_row, row, relay_row)
                relay_at = jnp.where(lat == busy_row, j, relay_at)

    def served_row(j):
        row = jnp.int32(0)
        for at, rows_served in order.items():
            row = jnp.where(lat == at, pick(j, rows_served), row)
        return row

    def busy(work):
        if idle is None:
            work()
        else:
            pl.when(active)(work)

    def resting(work):
        if idle is not None:
            pl.when(resting_now)(work)

    barrier = pltpu.get_barrier_semaphore()

    def greet(who):
        pl.semaphore_signal(barrier, inc=1, device_id=who, device_id_type=MESH)

    greet(twin)

    @busy
    def _():
        greet({"lon": ahead_lon})
        greet({"lon": behind_lon})
        if idle is not None:
            for at in (lon, ahead_lon, behind_lon):
                greet({"lat": relay_row, "lon": at})

    @resting
    def _():
        for j in range(others):
            for at in (lon, ahead_lon, behind_lon):
                greet({"lat": served_row(j), "lon": at})

    chosen = {}
    for side, (way, _) in enumerate(ways):
        hits = [leaves(plan_ref, chips, chip, t, way) for t in range(4)]
        for r in range(rounds):
            count, tile = jnp.int32(0), jnp.int32(0)
            for t in range(4):
                tile = jnp.where(hits[t] & (count == r), t, tile)
                count = count + hits[t].astype(jnp.int32)
            chosen[side, r] = jnp.where(tile // 2 == core, 0, 2) + lax.rem(tile, 2)

    lane = lax.broadcasted_iota(jnp.int32, (STEP, lanes), 1)
    is_last = lane == lanes - 1
    is_first = lane == 0
    force = gradient_coef * weight_coef

    def solve(c, half, to_ref):
        def group(slot, _):
            row = pl.multiple_of(half * quarter + c * STEP, STEP)
            base = pl.multiple_of(slot * (2 * quarter) + row, STEP)
            turn = lax.rem(lanes - (2 * half + slot) * (lanes // 4), lanes)
            at = pl.ds(pl.multiple_of(c * STEP, STEP), STEP)
            edges = [pltpu.roll(lat_ref[q, at, :], turn, 1) for q in range(fields // 2)]
            wet_c = wet[pl.ds(base + 8, STEP), :]
            wet_e = wet[pl.ds(base + 9, STEP), :]
            wet_w = wet[pl.ds(base + 7, STEP), :]
            zonal = meridional = None
            upper = []
            rhs = []
            for k in range(levels):
                center = [padded[f, k, pl.ds(base + 8, STEP), :] * wet_c for f in range(fields)]
                u, v = center[2], center[3]
                grad_x, grad_y, value = [], [], []
                for f in range(fields):
                    e = padded[f, k, pl.ds(base + 9, STEP), :] * wet_e
                    w = padded[f, k, pl.ds(base + 7, STEP), :] * wet_w
                    edge = pltpu.roll(edges[f // 2], lanes - 2 - 2 * (f % 2 * levels + k), 1)
                    n = jnp.where(is_last, edge, pltpu.roll(center[f], lanes - 1, 1))
                    s = jnp.where(is_first, edge, pltpu.roll(center[f], 1, 1))
                    gx, gy = e - w, n - s
                    grad_x.append(gx)
                    grad_y.append(gy)
                    total = (e + w) + (n + s)
                    flow = u * gx + v * gy
                    value.append(
                        (1.0 - 4.0 * diffuse_coef) * center[f] + (diffuse_coef * total - advect_coef * flow)
                    )
                dx = (force * haline_coef) * grad_x[1] - (force * thermal_coef) * grad_x[0]
                dy = (force * haline_coef) * grad_y[1] - (force * thermal_coef) * grad_y[0]
                zonal = dx if k == 0 else zonal + dx
                meridional = dy if k == 0 else meridional + dy
                value[2] = value[2] - zonal
                value[3] = value[3] - meridional
                lower_k = diff_ref[k - 1, pl.ds(base, STEP), :] if k > 0 else None
                upper_k = diff_ref[k, pl.ds(base, STEP), :] if k < levels - 1 else None
                pivot = 1.0
                if k > 0:
                    pivot = pivot + lower_k
                if k < levels - 1:
                    pivot = pivot + upper_k
                if k > 0:
                    pivot = pivot - lower_k * upper[k - 1]
                inverse = 1.0 / pivot
                upper.append(upper_k * inverse if k < levels - 1 else None)
                if k > 0:
                    value = [value[f] + lower_k * rhs[k - 1][f] for f in range(fields)]
                rhs.append([value[f] * inverse for f in range(fields)])
            for f in range(fields):
                x = rhs[levels - 1][f]
                to_ref[c, slot, f * levels + levels - 1] = x * wet_c
                for k in range(levels - 2, -1, -1):
                    x = rhs[k][f] + upper[k] * x
                    to_ref[c, slot, f * levels + k] = x * wet_c
            return 0

        lax.fori_loop(0, 2, group, 0, unroll=2)

    def first(c):
        return remote_copy(theirs.at[c], other.at[c], half_send.at[c, 0], half_recv.at[c, 0], twin)

    def second(c):
        return remote_copy(mine.at[c], other_theirs.at[c], half_send.at[c, 1], half_recv.at[c, 1], twin)

    def direct(c, side, r, part):
        return remote_copy(
            leaving.at[side, r, c, part],
            arrived.at[side, r, c, part],
            tile_send.at[c, side, r],
            tile_recv.at[c, side, r],
            {"lon": ways[side][1]},
        )

    def swap(c, side, r):
        return remote_copy(
            arrived.at[side, r, c],
            swapped.at[side, r, c],
            swap_send.at[c, side, r],
            swap_recv.at[c, side, r],
            twin,
        )


    def part_of(n):
        return n // RELAYED, pl.ds(lax.rem(n, RELAYED) * levels, levels)

    def detour(side, n):
        j = relay_at
        c, part = part_of(n)
        return remote_copy(
            leaving.at[side, 0, c, part],
            relayed.at[j, side, n],
            leg_send.at[side, n],
            leg_recv.at[j, side, n],
            {"lat": relay_row, "lon": ways[side][1]},
        )

    def forward(j, side, n):
        c, part = part_of(n)
        return remote_copy(
            relayed.at[j, side, n],
            arrived.at[side, 0, c, part],
            relay_send.at[j, side, n],
            relay_recv.at[side, n],
            {"lat": served_row(j)},
        )

    def pass_on(t):
        groups = [len(group) for group in served[idle[0]]]
        before, j, n = 0, jnp.int32(0), jnp.int32(0)
        for number, size in enumerate(groups):
            at = jnp.maximum(t - before * relays, 0)
            inside = t >= before * relays
            j = jnp.where(inside, before + lax.rem(at, size), j)
            n = jnp.where(inside, at // size, n)
            before += size
        for side in range(2):
            here(j, side, n).wait_recv()
            forward(j, side, n).start()

    def here(j, side, n):
        return remote_copy(
            relayed.at[j, side, n], relayed.at[j, side, n], relay_send.at[j, side, n], leg_recv.at[j, side, n], twin
        )

    def each_part(c, work):
        if idle is None:
            work(slice(0, planes))
            return
        for number in range(RELAYED + 1):
            skipped = number * levels
            around = jnp.clip(relays - c * RELAYED, 0, RELAYED) == number
            pl.when(around)(functools.partial(work, pl.ds(skipped, planes - skipped)))

    def each_relay(c, work):
        if idle is None:
            return
        for f in range(RELAYED):
            n = c * RELAYED + f
            pl.when(n < relays)(functools.partial(work, n))

    def advance(c, _):
        solve(c, 1 - core, theirs)

        @pl.when(c == 0)
        def _():
            if idle is None:
                pl.semaphore_wait(barrier, 3)
            else:
                busy(lambda: pl.semaphore_wait(barrier, 6))
                resting(lambda: pl.semaphore_wait(barrier, 1 + 3 * others))

        first(c).start()
        solve(c, core, mine)

        @busy
        def _():
            first(c).wait_recv()

            def pack(i, _):
                held = [ref[c, slot, i] for ref in (mine, other) for slot in range(2)]
                for (side, r), index in chosen.items():
                    leaving[side, r, c, i] = pick(index, held)
                return 0

            lax.fori_loop(0, planes, pack, 0, unroll=16)
            def relay(n):
                for side in range(2):
                    detour(side, n).start()

            def send(part):
                for side, r in keys:
                    direct(c, side, r, part).start()

            each_relay(c, relay)
            each_part(c, send)

        second(c).start()

        @resting
        def _():
            @pl.when((c > 0) & (c - 1 < others * relays))
            def _():
                pass_on(c - 1)

        return 0

    lax.fori_loop(0, chunks, advance, 0)

    origin = []
    for slot in range(2):
        target = 2 * lon + slot
        source = jnp.int32(0)
        for shift in range(-3, 4):
            g = lax.rem(target + shift + tiles, tiles)
            source = jnp.where(plan_ref[g] == target, g, source)
        from_chip, t = source // 4, lax.rem(source, 4)
        at = jnp.where(t // 2 == core, 0, 2) + lax.rem(t, 2)
        for side, (way, _) in enumerate(ways):
            came = from_chip == lax.rem(chip - way + chips, chips)
            rank = jnp.int32(0)
            for q in range(3):
                hit = leaves(plan_ref, chips, from_chip, q, way) & (q < t)
                rank = rank + hit.astype(jnp.int32)
            at = jnp.where(came, 4 + side * rounds + jnp.minimum(rank, rounds - 1), at)
        origin.append(at)

    def place(c):
        second(c).wait_recv()
        resting(first(c).wait_recv)

        @busy
        def _():
            for key in keys:
                swap(c, *key).wait_recv()

        def level(k, _):
            for f in range(fields):
                i = f * levels + k
                for part in range(2):
                    near, far, came = (
                        (mine, other, arrived) if part == 0 else (theirs, other_theirs, swapped)
                    )
                    values = [ref[c, slot, i] for ref in (near, far) for slot in range(2)]
                    values += [came[side, r, c, i] for side, r in keys]
                    half = core if part == 0 else 1 - core
                    for slot in range(2):
                        row = pl.multiple_of(2 * quarter * slot + half * quarter + c * STEP, STEP)
                        out_ref[f, k, pl.ds(row, STEP), :] = pick(origin[slot], values)
            return 0

        lax.fori_loop(0, levels, level, 0, unroll=2)

    def chunk_at(step):
        if idle is None:
            return step
        arrival, sent = [], 0
        for c in range(chunks):
            around = min(max(relays - c * RELAYED, 0), RELAYED)
            sent += fields - around
            arrival.append([sent, (c * RELAYED + around) if around else 0])
        arrival = [max(here / sent, there / relays) for here, there in arrival]
        return pick(step, sorted(range(chunks), key=lambda c: arrival[c]))

    def finish(c):
        first(c).wait_send()
        second(c).wait_send()

        @busy
        def _():
            def sent(part):
                for key in keys:
                    direct(c, *key, part).wait_send()

            def sent_relay(n):
                for side in range(2):
                    detour(side, n).wait_send()

            each_part(c, sent)
            each_relay(c, sent_relay)
            for key in keys:
                swap(c, *key).wait_send()

    left = others * relays - (chunks - 1) if idle is not None else 0
    each_step = -(-left // chunks)

    def drain(step, _):
        @busy
        def _():
            @pl.when(step < chunks)
            def _():
                c = chunk_at(step)

                def receive(part):
                    for key in keys:
                        direct(c, *key, part).wait_recv()

                def receive_relay(n):
                    for side in range(2):
                        forward(0, side, n).wait_recv()

                each_part(c, receive)
                each_relay(c, receive_relay)
                for key in keys:
                    swap(c, *key).start()

        @resting
        def _():
            for more in range(each_step):
                t = step * each_step + more
                pl.when(t < left)(lambda: pass_on(chunks - 1 + t))

        @pl.when(step > 0)
        def _():
            place(chunk_at(step - 1))
            finish(chunk_at(step - 1))

        return 0

    lax.fori_loop(0, chunks + 1, drain, 0)

    @resting
    def _():
        def relay_sent(n, _):
            for side in range(2):
                for j in range(others):
                    forward(j, side, n).wait_send()
            return 0

        lax.fori_loop(0, relays, relay_sent, 0)


def move(rounds, idle, plan, padded, wet, diffusivity, lat_edges):
    fields, levels, rows, lanes = padded.shape
    rows = rows - 16
    bands = lax.axis_size("lat")
    chunks = rows // 4 // STEP
    planes = fields * levels
    others, relays = 1, 1
    if idle is not None:
        served, relays = relay_plan(idle, bands)
        others = sum(len(group) for group in served[idle[0]])
    near = pl.BlockSpec(memory_space=pltpu.VMEM)
    halves = pltpu.VMEM((chunks, 2, planes, STEP, lanes), F32)
    pieces = pltpu.VMEM((2, rounds, chunks, planes, STEP, lanes), F32)
    dma = pltpu.SemaphoreType.DMA
    number = rounds if idle is None else 4 + idle_sets(bands).index(idle)
    return pl.pallas_call(
        functools.partial(move_kernel, rounds, idle),
        in_specs=[pl.BlockSpec(memory_space=pltpu.SMEM), near, near, near, near],
        out_specs=near,
        out_shape=jax.ShapeDtypeStruct((fields, levels, rows, lanes), F32),
        scratch_shapes=[
            halves,
            halves,
            halves,
            halves,
            pieces,
            pieces,
            pieces,
            pltpu.VMEM((others, 2, relays, levels, STEP, lanes), F32),
            dma((chunks, 2)),
            dma((chunks, 2)),
            dma((chunks, 2, rounds)),
            dma((chunks, 2, rounds)),
            dma((chunks, 2, rounds)),
            dma((chunks, 2, rounds)),
            dma((2, relays)),
            dma((others, 2, relays)),
            dma((others, 2, relays)),
            dma((2, relays)),
        ],
        compiler_params=pltpu.CompilerParams(
            collective_id=number, has_side_effects=True, vmem_limit_bytes=(24 + 6 * rounds) * MIB
        ),
    )(plan, padded, wet, diffusivity, lat_edges)


def local(relays, state, diffusivity, mask, tile_plan):
    plan = tile_plan.reshape(-1)
    lat_edges, padded, wet, diff, branch = halos(relays, plan, state, mask, diffusivity)
    branches = [functools.partial(move, rounds, None) for rounds in (1, 2, 3)]
    if relays:
        branches = [functools.partial(move, 1, idle) for idle in idle_sets(lax.axis_size("lat"))] + branches
    return lax.switch(branch[0], branches, plan, padded, wet, diff, lat_edges)


def solution(mesh):
    placed = (P(None, None, "lon", "lat"), P(None, "lon", "lat"), P("lon", "lat"), P(None, "lat"))
    relays = mesh.shape["lat"] == 4
    return jax.shard_map(
        functools.partial(local, relays),
        mesh=mesh,
        in_specs=placed,
        out_specs=P(None, None, "lon", "lat"),
        check_vma=False,
    )
```

```python
import functools

import jax
import jax.numpy as jnp
from jax import lax
from jax.experimental import pallas as pl
from jax.experimental.pallas import tpu as pltpu
from jax.sharding import PartitionSpec as P

advect_coef = 0.1
diffuse_coef = 0.1
gradient_coef = 0.1
thermal_coef = 0.2
haline_coef = 0.15
weight_coef = 0.25

F32 = jnp.float32
MIB = 1 << 20
MESH = pl.DeviceIdType.MESH
STEP = 8
RELAYED = 2


def relay_plan(idle, bands):
    busy = [row for row in range(bands) if row not in idle]
    if len(idle) == 1:
        row = idle[0]
        above, below = list(range(bands - 1, row, -1)), list(range(row))
        groups = []
        while above or below:
            groups.append([side.pop(0) for side in (above, below) if side])
        return {row: groups}, 7
    if idle[1] < busy[0] or busy[1] < idle[0]:
        return {idle[0]: [[busy[1]]], idle[1]: [[busy[0]]]}, 10
    return {idle[0]: [[busy[0]]], idle[1]: [[busy[1]]]}, 15


def idle_sets(bands):
    single = [(row,) for row in range(bands)]
    return single + [(a, b) for a in range(bands) for b in range(a + 1, bands)]


def remote_copy(source, target, send, recv, who):
    return pltpu.make_async_remote_copy(
        src_ref=source, dst_ref=target, send_sem=send, recv_sem=recv, device_id=who, device_id_type=MESH
    )


def halo_kernel(
    relays,
    plan_ref,
    state_ref,
    mask_ref,
    diff_ref,
    lat_ref,
    padded,
    wet,
    diff_out,
    branch_ref,
    mask,
    lat_pack,
    lon_pack,
    north_in,
    south_in,
    west_in,
    east_in,
    count,
    counts_in,
    load_sem,
    send_sem,
    recv_sem,
):
    fields, levels, rows, lanes = state_ref.shape
    half, quarter = rows // 2, rows // 4
    pairs = fields // 2
    width = lanes // 4
    lane = lax.broadcasted_iota(jnp.int32, (8, lanes), 1)
    devices, bands = lax.axis_size("lon"), lax.axis_size("lat")
    lon, lat = lax.axis_index("lon"), lax.axis_index("lat")
    top = lat == bands - 1
    to_east = {"lon": lax.rem(lon + 1, devices)}
    to_west = {"lon": lax.rem(lon + devices - 1, devices)}
    across = {"lon": devices - 1 - lon}
    others = [{"lat": lax.rem(lat + o, bands)} for o in range(1, bands)]
    barrier = pltpu.get_barrier_semaphore()
    for who in [to_east, to_west, across] + others:
        pl.semaphore_signal(barrier, inc=1, device_id=who, device_id_type=MESH)

    mask_load = pltpu.make_async_copy(mask_ref, mask, load_sem.at[fields])
    mask_load.start()
    loads = [
        pltpu.make_async_copy(state_ref.at[f], padded.at[f, :, pl.ds(8, rows), :], load_sem.at[f])
        for f in range(fields)
    ]
    for load in loads:
        load.start()
    diff_load = pltpu.make_async_copy(diff_ref, diff_out, load_sem.at[fields + 1])

    chips = devices // 2

    def leaving(chip, most):
        for way in (1, -1):
            number = jnp.int32(0)
            for t in range(4):
                number = number + leaves(plan_ref, chips, chip, t, way).astype(jnp.int32)
            most = jnp.maximum(most, number)
        return most

    most = lax.fori_loop(0, chips, leaving, jnp.int32(0))
    count[...] = jnp.full(count.shape, most, jnp.int32)

    def remote(source, target, at, recv_at, who):
        return remote_copy(source, target, send_sem.at[at], recv_sem.at[recv_at], who)

    north_who, south_who = {"lat": jnp.minimum(lat + 1, bands - 1)}, {"lat": jnp.maximum(lat - 1, 0)}
    up = [remote(lat_pack.at[q], south_in.at[q], q, q, north_who) for q in range(pairs)]
    down = [remote(lat_pack.at[q], north_in.at[q], pairs + q, pairs + q, south_who) for q in range(pairs)]
    fold = [remote(lat_pack.at[q], north_in.at[q], q, pairs + q, across) for q in range(pairs)]
    at_lon = 2 * pairs
    east = remote(lon_pack.at[1], west_in, at_lon, at_lon, to_east)
    west = remote(lon_pack.at[0], east_in, at_lon + 1, at_lon + 1, to_west)
    tell = [
        remote(count, counts_in.at[o], at_lon + 2 + o, at_lon + 2 + o, who) for o, who in enumerate(others)
    ]
    pl.semaphore_wait(barrier, 3 + bands - 1)
    for t in tell:
        t.start()
    mask_load.wait()
    wet[pl.ds(8, rows), :] = mask[...].astype(F32)
    wet[0:8, :] = jnp.ones((8, lanes), F32)
    wet[rows + 8 : rows + 16, :] = jnp.ones((8, lanes), F32)
    for q in range(pairs):
        pair = (2 * q, 2 * q + 1)
        for f in pair:
            loads[f].wait()

        def group(g, _):
            blocks = []
            for h in range(2):
                for slot in range(2):
                    at = pl.ds(pl.multiple_of(slot * half + h * quarter + g * 8 + 8, 8), 8)
                    cover = wet[at, :]
                    block = jnp.zeros((8, lanes), F32)
                    for f in pair:
                        for k in range(levels):
                            place = (2 * h + slot) * width + 2 * ((f - 2 * q) * levels + k)
                            x = pltpu.roll(padded[f, k, at, :] * cover, place + 1, 1)
                            block = jnp.where((lane >> 1) == (place >> 1), x, block)
                    blocks.append(block)
            to = pl.ds(pl.multiple_of(g * 8, 8), 8)
            lower = jnp.where(lane < width, blocks[0], blocks[1])
            upper = jnp.where(lane < 3 * width, blocks[2], blocks[3])
            lat_pack[q, to, :] = jnp.where(lane < 2 * width, lower, upper)
            return 0

        lax.fori_loop(0, quarter // 8, group, 0, unroll=4)
        pl.when(top)(fold[q].start)
        pl.when(jnp.logical_not(top))(up[q].start)
        pl.when(lat > 0)(down[q].start)

    diff_load.start()
    first = wet[8:9, :]
    final = wet[rows + 7 : rows + 8, :]
    for f in range(fields):
        at_field = slice(f * levels, (f + 1) * levels)
        lon_pack[0, at_field, :] = jnp.concatenate([padded[f, k, 8:9, :] for k in range(levels)], 0) * first
        lon_pack[1, at_field, :] = (
            jnp.concatenate([padded[f, k, rows + 7 : rows + 8, :] for k in range(levels)], 0) * final
        )
    east.start()
    west.start()

    values = [count[...]]
    value_rows = [lat]
    for o, t in enumerate(tell):
        t.wait_recv()
        values.append(counts_in[o])
        value_rows.append(lax.rem(lat + bands - o - 1, bands))
    largest = values[0]
    for value in values[1:]:
        largest = jnp.maximum(largest, value)
    branch = jnp.maximum(largest, 1) - 1
    if relays:
        sets = idle_sets(bands)
        branch = branch + len(sets)
        rests = []
        for row in range(bands):
            at_rest = jnp.zeros(count.shape, jnp.int32)
            for value, value_row in zip(values, value_rows):
                at_rest = jnp.where((value == 0) & (value_row == row), 1, at_rest)
            rests.append(at_rest == 1)
        for number, rows_at_rest in enumerate(sets):
            all_rest = functools.reduce(jnp.logical_and, [rests[row] for row in rows_at_rest])
            branch = jnp.where(all_rest & (largest <= 1), number, branch)
    branch_ref[0] = jnp.max(branch)
    east.wait_recv()
    west.wait_recv()
    for f in range(fields):
        for k in range(levels):
            i = f * levels + k
            padded[f, k, 7:8, :] = west_in[i : i + 1, :]
            padded[f, k, rows + 8 : rows + 9, :] = east_in[i : i + 1, :]

    @pl.when(lat > 0)
    def _():
        for copy in up:
            copy.wait_recv()

    @pl.when(lat == 0)
    def _():
        south_in[...] = jnp.zeros_like(south_in)

    for copy in down:
        copy.wait_recv()
    sub = lax.broadcasted_iota(jnp.int32, (8, lanes), 0)
    odd = (lane & 1) == 1
    outer = (lane // width) % 2 == 1
    groups = quarter // 8
    for q in range(pairs):
        sign = 1.0 if q == 0 else -1.0

        @pl.when(top)
        def _():
            for g in range(groups):
                x = north_in[q, (groups - 1 - g) * 8 : (groups - g) * 8, :]
                x = pltpu.roll(x, 4, 0)
                x = jnp.where((sub & 2) == 0, pltpu.roll(x, 6, 0), pltpu.roll(x, 2, 0))
                x = jnp.where((sub & 1) == 0, pltpu.roll(x, 7, 0), pltpu.roll(x, 1, 0))
                x = jnp.where(outer, pltpu.roll(x, 3 * width + 1, 1), pltpu.roll(x, width + 1, 1)) * sign
                south = pltpu.roll(south_in[q, g * 8 : g * 8 + 8, :], 2, 1)
                lat_ref[q, g * 8 : g * 8 + 8, :] = jnp.where(odd, x, south)

        @pl.when(jnp.logical_not(top))
        def _():
            for g in range(groups):
                south = pltpu.roll(south_in[q, g * 8 : g * 8 + 8, :], 2, 1)
                lat_ref[q, g * 8 : g * 8 + 8, :] = jnp.where(odd, north_in[q, g * 8 : g * 8 + 8, :], south)

    diff_load.wait()
    for q in range(pairs):
        up[q].wait_send()
        pl.when(lat > 0)(down[q].wait_send)
    east.wait_send()
    west.wait_send()
    for t in tell:
        t.wait_send()


def halos(relays, plan, state, mask, diffusivity):
    fields, levels, rows, lanes = state.shape
    bands = lax.axis_size("lat")
    pack = (fields // 2, rows // 4, lanes)
    edge = (fields * levels, lanes)
    near = pl.BlockSpec(memory_space=pltpu.VMEM)
    anywhere = pl.BlockSpec(memory_space=pl.ANY)
    scalars = pl.BlockSpec(memory_space=pltpu.SMEM)
    return pl.pallas_call(
        functools.partial(halo_kernel, relays),
        in_specs=[scalars, anywhere, anywhere, anywhere],
        out_specs=[near, near, near, near, scalars],
        out_shape=[
            jax.ShapeDtypeStruct(pack, F32),
            jax.ShapeDtypeStruct((fields, levels, rows + 16, lanes), F32),
            jax.ShapeDtypeStruct((rows + 16, lanes), F32),
            jax.ShapeDtypeStruct(diffusivity.shape, F32),
            jax.ShapeDtypeStruct((1,), jnp.int32),
        ],
        scratch_shapes=[
            pltpu.VMEM(mask.shape, jnp.int32),
            pltpu.VMEM(pack, F32),
            pltpu.VMEM((2,) + edge, F32),
            pltpu.VMEM(pack, F32),
            pltpu.VMEM(pack, F32),
            pltpu.VMEM(edge, F32),
            pltpu.VMEM(edge, F32),
            pltpu.VMEM((8, lanes), jnp.int32),
            pltpu.VMEM((bands - 1, 8, lanes), jnp.int32),
            pltpu.SemaphoreType.DMA((fields + 2,)),
            pltpu.SemaphoreType.DMA((fields + 2 + bands - 1,)),
            pltpu.SemaphoreType.DMA((fields + 2 + bands - 1,)),
        ],
        compiler_params=pltpu.CompilerParams(
            collective_id=0, has_side_effects=True, vmem_limit_bytes=55 * MIB
        ),
    )(plan, state, mask, diffusivity)


def leaves(plan_ref, chips, chip, t, way):
    target = plan_ref[4 * chip + t] // 4
    return target == lax.rem(chip + way + chips, chips)


def pick(index, values):
    chosen = values[0]
    for at, value in enumerate(values[1:], 1):
        chosen = jnp.where(index == at, value, chosen)
    return chosen


def move_kernel(
    rounds,
    idle,
    plan_ref,
    padded,
    wet,
    diff_ref,
    lat_ref,
    out_ref,
    mine,
    theirs,
    other,
    other_theirs,
    leaving,
    arrived,
    swapped,
    relayed,
    half_send,
    half_recv,
    tile_send,
    tile_recv,
    swap_send,
    swap_recv,
    leg_send,
    leg_recv,
    relay_send,
    relay_recv,
):
    fields, levels, rows, lanes = out_ref.shape
    planes = fields * levels
    quarter = rows // 4
    chunks = quarter // STEP
    devices, bands = lax.axis_size("lon"), lax.axis_size("lat")
    chips = devices // 2
    tiles = 4 * chips
    lon, lat = lax.axis_index("lon"), lax.axis_index("lat")
    chip, core = lon // 2, lax.rem(lon, 2)
    twin = {"lon": lon + 1 - 2 * core}
    ahead_lon = lax.rem(lon + 2, devices)
    behind_lon = lax.rem(lon + devices - 2, devices)
    ways = ((1, ahead_lon), (-1, behind_lon))
    keys = [(side, r) for side in range(2) for r in range(rounds)]
    if idle is None:
        served, relays, active, resting_now = {}, 0, None, None
    else:
        served, relays = relay_plan(idle, bands)
        resting_now = functools.reduce(jnp.logical_or, [lat == row for row in idle])
        active = jnp.logical_not(resting_now)
        order = {row: sum(groups, []) for row, groups in served.items()}
        others = len(order[idle[0]])
        relay_row, relay_at = jnp.int32(0), jnp.int32(0)
        for row, rows_served in order.items():
            for j, busy_row in enumerate(rows_served):
                relay_row = jnp.where(lat == busy_row, row, relay_row)
                relay_at = jnp.where(lat == busy_row, j, relay_at)

    def served_row(j):
        row = jnp.int32(0)
        for at, rows_served in order.items():
            row = jnp.where(lat == at, pick(j, rows_served), row)
        return row

    def busy(work):
        if idle is None:
            work()
        else:
            pl.when(active)(work)

    def resting(work):
        if idle is not None:
            pl.when(resting_now)(work)

    barrier = pltpu.get_barrier_semaphore()

    def greet(who):
        pl.semaphore_signal(barrier, inc=1, device_id=who, device_id_type=MESH)

    greet(twin)

    @busy
    def _():
        greet({"lon": ahead_lon})
        greet({"lon": behind_lon})
        if idle is not None:
            for at in (lon, ahead_lon, behind_lon):
                greet({"lat": relay_row, "lon": at})

    @resting
    def _():
        for j in range(others):
            for at in (lon, ahead_lon, behind_lon):
                greet({"lat": served_row(j), "lon": at})

    chosen = {}
    for side, (way, _) in enumerate(ways):
        hits = [leaves(plan_ref, chips, chip, t, way) for t in range(4)]
        for r in range(rounds):
            count, tile = jnp.int32(0), jnp.int32(0)
            for t in range(4):
                tile = jnp.where(hits[t] & (count == r), t, tile)
                count = count + hits[t].astype(jnp.int32)
            chosen[side, r] = jnp.where(tile // 2 == core, 0, 2) + lax.rem(tile, 2)

    lane = lax.broadcasted_iota(jnp.int32, (STEP, lanes), 1)
    is_last = lane == lanes - 1
    is_first = lane == 0
    force = gradient_coef * weight_coef

    def solve(c, half, to_ref):
        def group(slot, _):
            row = pl.multiple_of(half * quarter + c * STEP, STEP)
            base = pl.multiple_of(slot * (2 * quarter) + row, STEP)
            turn = lax.rem(lanes - (2 * half + slot) * (lanes // 4), lanes)
            at = pl.ds(pl.multiple_of(c * STEP, STEP), STEP)
            edges = [pltpu.roll(lat_ref[q, at, :], turn, 1) for q in range(fields // 2)]
            wet_c = wet[pl.ds(base + 8, STEP), :]
            wet_e = wet[pl.ds(base + 9, STEP), :]
            wet_w = wet[pl.ds(base + 7, STEP), :]
            zonal = meridional = None
            upper = []
            rhs = []
            for k in range(levels):
                center = [padded[f, k, pl.ds(base + 8, STEP), :] * wet_c for f in range(fields)]
                u, v = center[2], center[3]
                grad_x, grad_y, value = [], [], []
                for f in range(fields):
                    e = padded[f, k, pl.ds(base + 9, STEP), :] * wet_e
                    w = padded[f, k, pl.ds(base + 7, STEP), :] * wet_w
                    edge = pltpu.roll(edges[f // 2], lanes - 2 - 2 * (f % 2 * levels + k), 1)
                    n = jnp.where(is_last, edge, pltpu.roll(center[f], lanes - 1, 1))
                    s = jnp.where(is_first, edge, pltpu.roll(center[f], 1, 1))
                    gx, gy = e - w, n - s
                    grad_x.append(gx)
                    grad_y.append(gy)
                    total = (e + w) + (n + s)
                    flow = u * gx + v * gy
                    value.append(
                        (1.0 - 4.0 * diffuse_coef) * center[f] + (diffuse_coef * total - advect_coef * flow)
                    )
                dx = (force * haline_coef) * grad_x[1] - (force * thermal_coef) * grad_x[0]
                dy = (force * haline_coef) * grad_y[1] - (force * thermal_coef) * grad_y[0]
                zonal = dx if k == 0 else zonal + dx
                meridional = dy if k == 0 else meridional + dy
                value[2] = value[2] - zonal
                value[3] = value[3] - meridional
                lower_k = diff_ref[k - 1, pl.ds(base, STEP), :] if k > 0 else None
                upper_k = diff_ref[k, pl.ds(base, STEP), :] if k < levels - 1 else None
                pivot = 1.0
                if k > 0:
                    pivot = pivot + lower_k
                if k < levels - 1:
                    pivot = pivot + upper_k
                if k > 0:
                    pivot = pivot - lower_k * upper[k - 1]
                inverse = 1.0 / pivot
                upper.append(upper_k * inverse if k < levels - 1 else None)
                if k > 0:
                    value = [value[f] + lower_k * rhs[k - 1][f] for f in range(fields)]
                rhs.append([value[f] * inverse for f in range(fields)])
            for f in range(fields):
                x = rhs[levels - 1][f]
                to_ref[c, slot, f * levels + levels - 1] = x * wet_c
                for k in range(levels - 2, -1, -1):
                    x = rhs[k][f] + upper[k] * x
                    to_ref[c, slot, f * levels + k] = x * wet_c
            return 0

        lax.fori_loop(0, 2, group, 0, unroll=2)

    def first(c):
        return remote_copy(theirs.at[c], other.at[c], half_send.at[c, 0], half_recv.at[c, 0], twin)

    def second(c):
        return remote_copy(mine.at[c], other_theirs.at[c], half_send.at[c, 1], half_recv.at[c, 1], twin)

    def direct(c, side, r, part):
        return remote_copy(
            leaving.at[side, r, c, part],
            arrived.at[side, r, c, part],
            tile_send.at[c, side, r],
            tile_recv.at[c, side, r],
            {"lon": ways[side][1]},
        )

    def swap(c, side, r):
        return remote_copy(
            arrived.at[side, r, c],
            swapped.at[side, r, c],
            swap_send.at[c, side, r],
            swap_recv.at[c, side, r],
            twin,
        )


    def part_of(n):
        return n // RELAYED, pl.ds(lax.rem(n, RELAYED) * levels, levels)

    def detour(side, n):
        j = relay_at
        c, part = part_of(n)
        return remote_copy(
            leaving.at[side, 0, c, part],
            relayed.at[j, side, n],
            leg_send.at[side, n],
            leg_recv.at[j, side, n],
            {"lat": relay_row, "lon": ways[side][1]},
        )

    def forward(j, side, n):
        c, part = part_of(n)
        return remote_copy(
            relayed.at[j, side, n],
            arrived.at[side, 0, c, part],
            relay_send.at[j, side, n],
            relay_recv.at[side, n],
            {"lat": served_row(j)},
        )

    def pass_on(t):
        groups = [len(group) for group in served[idle[0]]]
        before, j, n = 0, jnp.int32(0), jnp.int32(0)
        for number, size in enumerate(groups):
            at = jnp.maximum(t - before * relays, 0)
            inside = t >= before * relays
            j = jnp.where(inside, before + lax.rem(at, size), j)
            n = jnp.where(inside, at // size, n)
            before += size
        for side in range(2):
            here(j, side, n).wait_recv()
            forward(j, side, n).start()

    def here(j, side, n):
        return remote_copy(
            relayed.at[j, side, n], relayed.at[j, side, n], relay_send.at[j, side, n], leg_recv.at[j, side, n], twin
        )

    def each_part(c, work):
        if idle is None:
            work(slice(0, planes))
            return
        for number in range(RELAYED + 1):
            skipped = number * levels
            around = jnp.clip(relays - c * RELAYED, 0, RELAYED) == number
            pl.when(around)(functools.partial(work, pl.ds(skipped, planes - skipped)))

    def each_relay(c, work):
        if idle is None:
            return
        for f in range(RELAYED):
            n = c * RELAYED + f
            pl.when(n < relays)(functools.partial(work, n))

    def advance(c, _):
        solve(c, 1 - core, theirs)

        @pl.when(c == 0)
        def _():
            if idle is None:
                pl.semaphore_wait(barrier, 3)
            else:
                busy(lambda: pl.semaphore_wait(barrier, 6))
                resting(lambda: pl.semaphore_wait(barrier, 1 + 3 * others))

        first(c).start()
        solve(c, core, mine)

        @busy
        def _():
            first(c).wait_recv()

            def pack(i, _):
                held = [ref[c, slot, i] for ref in (mine, other) for slot in range(2)]
                for (side, r), index in chosen.items():
                    leaving[side, r, c, i] = pick(index, held)
                return 0

            lax.fori_loop(0, planes, pack, 0, unroll=16)
            def relay(n):
                for side in range(2):
                    detour(side, n).start()

            def send(part):
                for side, r in keys:
                    direct(c, side, r, part).start()

            each_relay(c, relay)
            each_part(c, send)

        second(c).start()

        @resting
        def _():
            @pl.when((c > 0) & (c - 1 < others * relays))
            def _():
                pass_on(c - 1)

        return 0

    lax.fori_loop(0, chunks, advance, 0)

    origin = []
    for slot in range(2):
        target = 2 * lon + slot
        source = jnp.int32(0)
        for shift in range(-3, 4):
            g = lax.rem(target + shift + tiles, tiles)
            source = jnp.where(plan_ref[g] == target, g, source)
        from_chip, t = source // 4, lax.rem(source, 4)
        at = jnp.where(t // 2 == core, 0, 2) + lax.rem(t, 2)
        for side, (way, _) in enumerate(ways):
            came = from_chip == lax.rem(chip - way + chips, chips)
            rank = jnp.int32(0)
            for q in range(3):
                hit = leaves(plan_ref, chips, from_chip, q, way) & (q < t)
                rank = rank + hit.astype(jnp.int32)
            at = jnp.where(came, 4 + side * rounds + jnp.minimum(rank, rounds - 1), at)
        origin.append(at)

    def place(c):
        second(c).wait_recv()
        resting(first(c).wait_recv)

        @busy
        def _():
            for key in keys:
                swap(c, *key).wait_recv()

        def level(k, _):
            for f in range(fields):
                i = f * levels + k
                for part in range(2):
                    near, far, came = (
                        (mine, other, arrived) if part == 0 else (theirs, other_theirs, swapped)
                    )
                    values = [ref[c, slot, i] for ref in (near, far) for slot in range(2)]
                    values += [came[side, r, c, i] for side, r in keys]
                    half = core if part == 0 else 1 - core
                    for slot in range(2):
                        row = pl.multiple_of(2 * quarter * slot + half * quarter + c * STEP, STEP)
                        out_ref[f, k, pl.ds(row, STEP), :] = pick(origin[slot], values)
            return 0

        lax.fori_loop(0, levels, level, 0, unroll=2)

    def chunk_at(step):
        if idle is None:
            return step
        arrival, sent = [], 0
        for c in range(chunks):
            around = min(max(relays - c * RELAYED, 0), RELAYED)
            sent += fields - around
            arrival.append([sent, (c * RELAYED + around) if around else 0])
        arrival = [max(here / sent, there / relays) for here, there in arrival]
        return pick(step, sorted(range(chunks), key=lambda c: arrival[c]))

    def finish(c):
        first(c).wait_send()
        second(c).wait_send()

        @busy
        def _():
            def sent(part):
                for key in keys:
                    direct(c, *key, part).wait_send()

            def sent_relay(n):
                for side in range(2):
                    detour(side, n).wait_send()

            each_part(c, sent)
            each_relay(c, sent_relay)
            for key in keys:
                swap(c, *key).wait_send()

    left = others * relays - (chunks - 1) if idle is not None else 0
    each_step = -(-left // chunks)

    def drain(step, _):
        @busy
        def _():
            @pl.when(step < chunks)
            def _():
                c = chunk_at(step)

                def receive(part):
                    for key in keys:
                        direct(c, *key, part).wait_recv()

                def receive_relay(n):
                    for side in range(2):
                        forward(0, side, n).wait_recv()

                each_part(c, receive)
                each_relay(c, receive_relay)
                for key in keys:
                    swap(c, *key).start()

        @resting
        def _():
            for more in range(each_step):
                t = step * each_step + more
                pl.when(t < left)(lambda: pass_on(chunks - 1 + t))

        @pl.when(step > 0)
        def _():
            place(chunk_at(step - 1))
            finish(chunk_at(step - 1))

        return 0

    lax.fori_loop(0, chunks + 1, drain, 0)

    @resting
    def _():
        def relay_sent(n, _):
            for side in range(2):
                for j in range(others):
                    forward(j, side, n).wait_send()
            return 0

        lax.fori_loop(0, relays, relay_sent, 0)


def move(rounds, idle, plan, padded, wet, diffusivity, lat_edges):
    fields, levels, rows, lanes = padded.shape
    rows = rows - 16
    bands = lax.axis_size("lat")
    chunks = rows // 4 // STEP
    planes = fields * levels
    others, relays = 1, 1
    if idle is not None:
        served, relays = relay_plan(idle, bands)
        others = sum(len(group) for group in served[idle[0]])
    near = pl.BlockSpec(memory_space=pltpu.VMEM)
    halves = pltpu.VMEM((chunks, 2, planes, STEP, lanes), F32)
    pieces = pltpu.VMEM((2, rounds, chunks, planes, STEP, lanes), F32)
    dma = pltpu.SemaphoreType.DMA
    number = rounds if idle is None else 4 + idle_sets(bands).index(idle)
    return pl.pallas_call(
        functools.partial(move_kernel, rounds, idle),
        in_specs=[pl.BlockSpec(memory_space=pltpu.SMEM), near, near, near, near],
        out_specs=near,
        out_shape=jax.ShapeDtypeStruct((fields, levels, rows, lanes), F32),
        scratch_shapes=[
            halves,
            halves,
            halves,
            halves,
            pieces,
            pieces,
            pieces,
            pltpu.VMEM((others, 2, relays, levels, STEP, lanes), F32),
            dma((chunks, 2)),
            dma((chunks, 2)),
            dma((chunks, 2, rounds)),
            dma((chunks, 2, rounds)),
            dma((chunks, 2, rounds)),
            dma((chunks, 2, rounds)),
            dma((2, relays)),
            dma((others, 2, relays)),
            dma((others, 2, relays)),
            dma((2, relays)),
        ],
        compiler_params=pltpu.CompilerParams(
            collective_id=number, has_side_effects=True, vmem_limit_bytes=(24 + 6 * rounds) * MIB
        ),
    )(plan, padded, wet, diffusivity, lat_edges)


def local(relays, state, diffusivity, mask, tile_plan):
    plan = tile_plan.reshape(-1)
    lat_edges, padded, wet, diff, branch = halos(relays, plan, state, mask, diffusivity)
    branches = [functools.partial(move, rounds, None) for rounds in (1, 2, 3)]
    if relays:
        branches = [functools.partial(move, 1, idle) for idle in idle_sets(lax.axis_size("lat"))] + branches
    return lax.switch(branch[0], branches, plan, padded, wet, diff, lat_edges)


def solution(mesh):
    placed = (P(None, None, "lon", "lat"), P(None, "lon", "lat"), P("lon", "lat"), P(None, "lat"))
    relays = mesh.shape["lat"] == 4
    return jax.shard_map(
        functools.partial(local, relays),
        mesh=mesh,
        in_specs=placed,
        out_specs=P(None, None, "lon", "lat"),
        check_vma=False,
    )
```
